32 devices in a mesh: dp: 16 (over z, y, x), section: 2 (over core).
Axes of the slice: x: 2, y: 2, z: 4, core: 2. Of those that a mesh axis runs over, the one named last changes fastest.
Arguments:
- tokens: bfloat16 [32768, 512], P('dp'), may hold values from -6 to 6
- cotangent: bfloat16 [32768, 512], P('dp'), may hold values from -6 to 6
- lengths: int32 [32], P('dp'), may hold values from 256 to 1024, as said below
- train_counts: int32 [32], P('dp'), may hold values from 65 to 768, as said below
- w_qkv: bfloat16 [2, 512, 1536], P('section'), may hold values from -0.25 to 0.25
- w_out: bfloat16 [2, 512, 512], P('section'), may hold values from -1.5 to 1.5
- w_up: bfloat16 [2, 512, 1024], P('section'), may hold values from -0.25 to 0.25
- b_up: float32 [2, 1024], P('section'), may hold values from -3 to 3
- w_down: bfloat16 [2, 1024, 512], P('section'), may hold values from -0.1875 to 0.1875
- b_down: float32 [2, 512], P('section'), may hold values from -3 to 3
- gain_one: float32 [2, 512], P('section'), may hold values from 0.1 to 1.9
- bias_one: float32 [2, 512], P('section'), may hold values from -3 to 3
- gain_two: float32 [2, 512], P('section'), may hold values from 0.1 to 1.9
- bias_two: float32 [2, 512], P('section'), may hold values from -3 to 3
Outputs:
- output: bfloat16 [32768, 512], P('dp', 'section')
- grad_tokens: bfloat16 [32768, 512], P('dp', 'section')
- grad_w_qkv: float32 [2, 512, 1536], P('section')
- grad_w_out: float32 [2, 512, 512], P('section')
- grad_w_up: float32 [2, 512, 1024], P('section')
- grad_b_up: float32 [2, 1024], P('section')
- grad_w_down: float32 [2, 1024, 512], P('section')
- grad_b_down: float32 [2, 512], P('section')
- grad_gain_one: float32 [2, 512], P('section')
- grad_bias_one: float32 [2, 512], P('section')
- grad_gain_two: float32 [2, 512], P('section')
- grad_bias_two: float32 [2, 512], P('section')
The draws below stay inside these ranges and needn't reach their ends.
Inputs may be any that keep to these rules, and one draw needn't show every extreme that they name: `lengths`: some dataset has 1024 samples and some has 256. `train_counts`: between a quarter (plus one) and three quarters of the dataset's samples; the training samples are its first slots.
All inputs are finite; a program needn't handle non-finite values.
Results may differ from the reference program's by a relative error of at most 0.034.
Values may be sent and summed in bfloat16 or wider, within the bound.
No kernel may reach another device: no remote copies, remote signals or barrier semaphores. Data moves between devices by JAX's collectives and lax.ppermute only.
A program may use at most 192 MiB of HBM per device.

```python
import jax
import jax.numpy as jnp
from jax import lax

D = 512
FF = 1024
HEAD_DIM = 128
SEQ = 1024
DATASETS = 32
TOKENS = 32768


def dataset_plan(key):
    drawn = jax.random.randint(key, (DATASETS,), SEQ // 4, SEQ + 1)
    chosen = jax.random.randint(jax.random.fold_in(key, 11), (), 0, DATASETS)
    shortest = (chosen + 1) % DATASETS
    places = jnp.arange(DATASETS)
    lengths = jnp.where(places == chosen, SEQ, jnp.where(places == shortest, SEQ // 4, drawn))
    return (lengths.astype(jnp.int32), places == chosen, places == shortest)


def draw_lengths(key, part):
    lengths, longest_mask, shortest_mask = dataset_plan(key)
    return lengths


def draw_train_counts(key, part):
    lengths, longest_mask, shortest_mask = dataset_plan(key)
    key = jax.random.fold_in(key, 2)
    drawn = jax.random.randint(key, (DATASETS,), lengths // 4 + 1, lengths * 3 // 4 + 1)
    counts = jnp.where(longest_mask, SEQ * 3 // 4, jnp.where(shortest_mask, SEQ // 4 // 4 + 1, drawn))
    return counts.astype(jnp.int32)


def block_scale(key, shape, split, least, high):
    loudness = 1.0
    for position, parts in split:
        heights = jax.random.uniform(jax.random.fold_in(jax.random.fold_in(key, 6), position), (parts,), jnp.float32, least / len(split), high / len(split))
        loudness = loudness * jnp.repeat(jnp.exp(heights), shape[position] // parts).reshape((-1,) + (1,) * (len(shape) - 1 - position))
    return loudness


def gaussian(own_key, shape, scale, limit, split=(), kind=jnp.bfloat16):
    gain = block_scale(own_key, shape, split, -0.22, 0.18) if split else 1.0
    array = jax.random.normal(own_key, shape, jnp.float32) * scale * gain
    return jnp.minimum(jnp.maximum(array, -limit), limit).astype(kind)


def setup_inputs(seed: int = 0) -> dict:
    seeds = jax.random.split(jax.random.key(seed), 15)
    return {
        "tokens": gaussian(seeds[0], (TOKENS, D), 1.0, 6.0, ((0, 16),)),
        "cotangent": gaussian(seeds[1], (TOKENS, D), 1.0, 6.0, ((0, 16),)),
        "lengths": draw_lengths(jax.random.fold_in(seeds[14], 71), 0),
        "train_counts": draw_train_counts(jax.random.fold_in(seeds[14], 71), 0),
        "w_qkv": gaussian(seeds[4], (2, D, 3 * D), D ** -0.5, 0.25, ((0, 2),)),
        "w_out": gaussian(seeds[5], (2, D, D), (D // 32) ** -0.5, 1.5, ((0, 2),)),
        "w_up": gaussian(seeds[6], (2, D, FF), D ** -0.5, 0.25, ((0, 2),)),
        "b_up": gaussian(seeds[7], (2, FF), 0.5, 3.0, ((0, 2),), jnp.float32),
        "w_down": gaussian(seeds[8], (2, FF, D), FF ** -0.5, 0.1875, ((0, 2),)),
        "b_down": gaussian(seeds[9], (2, D), 0.5, 3.0, ((0, 2),), jnp.float32),
        "gain_one": jnp.clip(1.0 + 0.18 * jax.random.normal(seeds[10], (2, D), jnp.float32), 0.1, 1.9),
        "bias_one": gaussian(seeds[11], (2, D), 0.5, 3.0, ((0, 2),), jnp.float32),
        "gain_two": jnp.clip(1.0 + 0.18 * jax.random.normal(seeds[12], (2, D), jnp.float32), 0.1, 1.9),
        "bias_two": gaussian(seeds[13], (2, D), 0.5, 3.0, ((0, 2),), jnp.float32),
    }


EPS = 1e-05
PRECISE = lax.Precision.HIGHEST

@jax.custom_vjp
def low(v):
    return lax.optimization_barrier(v.astype(jnp.bfloat16)).astype(jnp.float32)

@jax.custom_vjp
def low_back(v):
    return v

def low_keep(v):
    return (low(v), None)

def low_pass(kept, grad):
    return (grad,)

def back_keep(v):
    return (v, None)

def back_low(kept, grad):
    return (low(grad),)
low.defvjp(low_keep, low_pass)
low_back.defvjp(back_keep, back_low)

def layer_norm(entries, gain_vec, bias_vec):
    average = lax.optimization_barrier(jnp.mean(entries, axis=-1, keepdims=True))
    centred = entries - average
    spread = lax.optimization_barrier(jnp.mean(centred * centred, axis=-1, keepdims=True))
    return centred * lax.rsqrt(spread + EPS) * gain_vec + bias_vec

def product(left_side, right_side):
    return jnp.dot(left_side, right_side, precision=PRECISE)

def one_layer(inputs, key_valid, params):
    w_qkv, w_out, w_up, b_up, w_down, b_down, gain_one, bias_one, gain_two, bias_two = params
    seq_len, model_width = inputs.shape
    head_count = model_width // HEAD_DIM
    qkv_both = low_back(low(product(inputs, w_qkv)))
    split_qkv = qkv_both.reshape(seq_len, 3, head_count, HEAD_DIM)
    queries = split_qkv[:, 0]
    key_heads = split_qkv[:, 1]
    values = split_qkv[:, 2]
    scores = low_back(jnp.einsum('qhd,khd->hqk', queries, key_heads, precision=PRECISE) * HEAD_DIM ** (-0.5))
    scores = jnp.where(key_valid[None, None, :], scores, -1e+30)
    highest = lax.optimization_barrier(jnp.max(scores, axis=-1, keepdims=True))
    weights = jnp.exp(scores - highest)
    probs_now = low(weights / lax.optimization_barrier(jnp.sum(weights, axis=-1, keepdims=True)))
    mixed_heads = jnp.einsum('hqk,khd->qhd', probs_now, values, precision=PRECISE)
    mixed_low = low_back(low(mixed_heads.reshape(seq_len, model_width)))
    attn_out = low_back(product(mixed_low, w_out))
    hidden_one = layer_norm(inputs + attn_out, gain_one, bias_one)
    pre_act = low_back(product(low(hidden_one), w_up) + b_up)
    act_low = low(jax.nn.gelu(pre_act, approximate=True))
    summed = hidden_one + (low_back(product(act_low, w_down)) + b_down)
    return layer_norm(summed, gain_two, bias_two)

def sequence(tokens_seq, length_now, train_now, params):
    positions = jnp.arange(tokens_seq.shape[0])
    key_valid = positions < train_now
    first_out = one_layer(tokens_seq, key_valid, tuple((member[0] for member in params)))
    moved = low_back(low(first_out))
    second_out = one_layer(moved, key_valid, tuple((member[1] for member in params)))
    return second_out * (positions < length_now)[:, None].astype(second_out.dtype)

def reference(tokens, cotangent, lengths, train_counts, w_qkv, w_out, w_up, b_up, w_down, b_down, gain_one, bias_one, gain_two, bias_two):
    weights_in = (w_qkv, w_out, w_up, b_up, w_down, b_down, gain_one, bias_one, gain_two, bias_two)
    params = tuple((member.astype(jnp.float32) for member in weights_in))
    step_fn = jax.checkpoint(sequence)

    def forward(flat_tokens, params_in):
        batched = flat_tokens.reshape(DATASETS, SEQ, D)

        def scan_step(carry_val, items):
            return (carry_val, step_fn(items[0], items[1], items[2], params_in))
        _, outputs = lax.scan(scan_step, jnp.zeros((), jnp.float32), (batched, lengths, train_counts))
        return outputs.reshape(DATASETS * SEQ, D)
    outputs, pullback = jax.vjp(forward, tokens.astype(jnp.float32), params)
    grad_tokens, grad_params = pullback(cotangent.astype(jnp.float32))
    return (outputs.astype(jnp.bfloat16), grad_tokens.astype(jnp.bfloat16), grad_params[0], grad_params[1], grad_params[2], grad_params[3], grad_params[4], grad_params[5], grad_params[6], grad_params[7], grad_params[8], grad_params[9])
```

```python
import functools

import jax
import jax.numpy as jnp
from jax import lax
from jax.experimental import pallas as pl
from jax.experimental.pallas import tpu as pltpu
from jax.sharding import PartitionSpec as P

HEAD_DIM = 128
EPS = 1e-05
LOG2E = 1.4426950408889634
ROOT = 0.7978845608028654
CUBE = 0.044715
BF = jnp.bfloat16
F32 = jnp.float32
WIDTH = 512
TILE = 16
MIB = 1 << 20

IN_VMEM = pl.BlockSpec(memory_space=pltpu.VMEM)
IN_SMEM = pl.BlockSpec(memory_space=pltpu.SMEM)


def shape(dims, kind):
    return jax.ShapeDtypeStruct(dims, kind)


def call(kernel, name, outs, ins, scratch=(), limit=44, flops=0, moved=0):
    return pl.pallas_call(
        kernel,
        out_shape=outs,
        in_specs=ins,
        out_specs=jax.tree.map(lambda _: IN_VMEM, outs),
        scratch_shapes=list(scratch),
        compiler_params=pltpu.CompilerParams(vmem_limit_bytes=limit * MIB),
        cost_estimate=pl.CostEstimate(flops=flops, bytes_accessed=moved, transcendentals=0),
        name=name,
    )


def dot(left, right):
    return lax.dot_general(left, right, (((1,), (0,)), ((), ())), preferred_element_type=F32)


def dot_rt(left, right):
    return lax.dot_general(left, right, (((1,), (1,)), ((), ())), preferred_element_type=F32)


def dot_lt(left, right):
    return lax.dot_general(left, right, (((0,), (0,)), ((), ())), preferred_element_type=F32)


def mean(block):
    return jnp.mean(block, axis=1, keepdims=True)


def down(block):
    return jnp.sum(block, axis=0, keepdims=True)


def normed(block):
    centred = block - mean(block)
    scale = lax.rsqrt(mean(centred * centred) + EPS)
    return centred * scale, scale


def attend_kernel(keys, count_ref, u_ref, w_ref, q_ref, k_ref, v_ref, p_ref, mixed_ref):
    seq, width = u_ref.shape
    factor = HEAD_DIM**-0.5 * LOG2E
    k_ref[...] = dot(u_ref[0:keys], w_ref[:, width : 2 * width]).astype(BF)
    v_ref[...] = dot(u_ref[0:keys], w_ref[:, 2 * width :]).astype(BF)
    q_ref[...] = dot(u_ref[...], w_ref[:, :width]).astype(BF)
    places = lax.broadcasted_iota(jnp.int32, (1, keys), 1)
    bias = jnp.where(places < count_ref[0], 0.0, -1e30).astype(F32)
    for head in range(width // HEAD_DIM):
        cols = slice(head * HEAD_DIM, (head + 1) * HEAD_DIM)
        scores = dot_rt(q_ref[:, cols], k_ref[:, cols]) * factor + bias
        powers = jnp.exp2(scores - jnp.max(scores, axis=1, keepdims=True))
        total = jnp.sum(powers, axis=1, keepdims=True)
        probs = (powers * (1.0 / total)).astype(BF)
        p_ref[head] = probs
        mixed_ref[:, cols] = dot(probs, v_ref[:, cols]).astype(BF)


def attend(count, u, w_qkv):
    seq, width = u.shape
    keys = seq * 3 // 4
    return call(
        functools.partial(attend_kernel, keys),
        "attend",
        [
            shape((seq, width), BF),
            shape((keys, width), BF),
            shape((keys, width), BF),
            shape((width // HEAD_DIM, seq, keys), BF),
            shape((seq, width), BF),
        ],
        [IN_SMEM, IN_VMEM, IN_VMEM],
        flops=8_000_000_000,
        moved=10_000_000,
    )(count, u, w_qkv)


def feed_kernel(
    vec_ref, u_ref, mixed_ref, w_out_ref, w_up_ref, w_down_ref,
    x1_ref, s1_ref, h_ref, g_ref, slope_ref, x2_ref, s2_ref, y_ref,
):
    hidden = w_up_ref.shape[1]
    vec = vec_ref[...]
    half = WIDTH
    a = u_ref[...].astype(F32) + dot(mixed_ref[...], w_out_ref[...])
    x1, s1 = normed(a)
    x1_ref[...] = x1.astype(BF)
    s1_ref[...] = s1
    h = x1 * vec[3:4] + vec[4:5]
    h_low = h.astype(BF)
    h_ref[...] = h_low
    f = h + vec[2:3]
    for part in range(hidden // half):
        cols = slice(part * half, (part + 1) * half)
        z = dot(h_low, w_up_ref[:, cols]) + vec[part : part + 1]
        square = z * z
        curve = jnp.tanh(z * (ROOT + ROOT * CUBE * square))
        gate = 0.5 * curve + 0.5
        g = (z * gate).astype(BF)
        g_ref[:, cols] = g
        slope = gate + (0.5 * z) * (1.0 - curve * curve) * (ROOT + 3 * ROOT * CUBE * square)
        slope_ref[:, cols] = slope.astype(BF)
        f = f + dot(g, w_down_ref[cols])
    x2, s2 = normed(f)
    x2_ref[...] = x2.astype(BF)
    s2_ref[...] = s2
    y_ref[...] = (x2 * vec[5:6] + vec[6:7]).astype(BF)


def feed(vec, u, mixed, w_out, w_up, w_down):
    seq, width = u.shape
    hidden = w_up.shape[1]
    return call(
        feed_kernel,
        "feed",
        [
            shape((seq, width), BF),
            shape((seq, 1), F32),
            shape((seq, width), BF),
            shape((seq, hidden), BF),
            shape((seq, hidden), BF),
            shape((seq, width), BF),
            shape((seq, 1), F32),
            shape((seq, width), BF),
        ],
        [IN_VMEM] * 6,
        flops=7_000_000_000,
        moved=10_000_000,
    )(vec, u, mixed, w_out, w_up, w_down)


def feed_back_kernel(
    info_ref, vec_ref, dy_ref, x2_ref, s2_ref, g_ref, slope_ref, h_ref, x1_ref, s1_ref, mixed_ref,
    w_down_ref, w_up_ref, w_out_ref,
    send_ref, keep_ref, dm_ref, da_ref,
    df_ref, dz_ref, total_ref,
):
    seq, width = dy_ref.shape
    hidden = w_up_ref.shape[1]
    half = WIDTH
    vec = vec_ref[...]
    rows = lax.broadcasted_iota(jnp.int32, (seq, 1), 0)
    dy = dy_ref[...].astype(F32) * (rows < info_ref[1]).astype(F32)
    x2 = x2_ref[...].astype(F32)
    small = [None] * 7
    small[6] = down(dy)
    small[5] = down(dy * x2)
    t = dy * vec[5:6]
    df = s2_ref[...] * (t - mean(t) - x2 * mean(t * x2))
    small[2] = down(df)
    df_low = df.astype(BF)
    df_ref[...] = df_low
    dh = df
    for part in range(hidden // half):
        cols = slice(part * half, (part + 1) * half)
        dz = (dot_rt(df_low, w_down_ref[cols]) * slope_ref[:, cols].astype(F32)).astype(BF)
        dz_ref[:, cols] = dz
        small[part] = down(dz.astype(F32))
        dh = dh + dot_rt(dz, w_up_ref[:, cols])
    x1 = x1_ref[...].astype(F32)
    small[4] = down(dh)
    small[3] = down(dh * x1)
    t = dh * vec[3:4]
    da = (s1_ref[...] * (t - mean(t) - x1 * mean(t * x1))).astype(BF)
    da_ref[...] = da
    dm_ref[...] = dot_rt(da, w_out_ref[...]).astype(BF)
    total_ref[0:hidden] = dot_lt(g_ref[...], df_low).astype(BF)
    for part in range(hidden // half):
        cols = slice(part * half, (part + 1) * half)
        total_ref[hidden + part * width : hidden + (part + 1) * width] = dot_lt(
            h_ref[...], dz_ref[:, cols]
        ).astype(BF)
    last = hidden + hidden // half * width
    total_ref[last : last + width] = dot_lt(mixed_ref[...], da).astype(BF)
    share_out(info_ref, total_ref, send_ref, keep_ref)
    bottom = jnp.concatenate(small + [jnp.zeros((TILE - 7, width), F32)], axis=0).astype(BF)
    send_ref[total_ref.shape[0] // 2 :] = bottom
    keep_ref[total_ref.shape[0] // 2 :] = bottom


def share_out(info_ref, total_ref, send_ref, keep_ref):
    half = total_ref.shape[0] // 2
    mine = info_ref[0] * half
    keep_ref[0:half] = total_ref[pl.ds(pl.multiple_of(mine, TILE), half)]
    send_ref[0:half] = total_ref[pl.ds(pl.multiple_of(half - mine, TILE), half)]


def feed_back(info, vec, dy, x2, s2, g, slope, h, x1, s1, mixed, w_down, w_up, w_out):
    seq, width = dy.shape
    hidden = w_up.shape[1]
    rows = 2 * hidden + width
    return call(
        feed_back_kernel,
        "feed_back",
        [
            shape((rows // 2 + TILE, width), BF),
            shape((rows // 2 + TILE, width), BF),
            shape((seq, width), BF),
            shape((seq, width), BF),
        ],
        [IN_SMEM] + [IN_VMEM] * 13,
        scratch=[
            pltpu.VMEM((seq, width), BF),
            pltpu.VMEM((seq, hidden), BF),
            pltpu.VMEM((rows, width), BF),
        ],
        flops=12_000_000_000,
        moved=16_000_000,
    )(info, vec, dy, x2, s2, g, slope, h, x1, s1, mixed, w_down, w_up, w_out)


def attend_back_kernel(
    info_ref, q_ref, k_ref, v_ref, p_ref, mixed_ref, dm_ref, u_ref,
    send_ref, keep_ref, dqkv_ref,
    total_ref,
):
    seq, width = u_ref.shape
    keys = k_ref.shape[0]
    scale = HEAD_DIM**-0.5
    for head in range(width // HEAD_DIM):
        cols = slice(head * HEAD_DIM, (head + 1) * HEAD_DIM)
        dm = dm_ref[:, cols]
        inner = jnp.sum(dm.astype(F32) * mixed_ref[:, cols].astype(F32), axis=1, keepdims=True)
        probs = p_ref[head]
        ds = (probs.astype(F32) * (dot_rt(dm, v_ref[:, cols]) - inner)).astype(BF)
        dqkv_ref[:, cols] = (dot(ds, k_ref[:, cols]) * scale).astype(BF)
        dk = (dot(q_ref[:, cols].T, ds) * scale).T
        dv = dot(dm.T, probs).T
        dqkv_ref[0:keys, width + head * HEAD_DIM : width + (head + 1) * HEAD_DIM] = dk.astype(BF)
        dqkv_ref[0:keys, 2 * width + head * HEAD_DIM : 2 * width + (head + 1) * HEAD_DIM] = (
            dv.astype(BF)
        )
    dqkv_ref[keys:seq, width:] = jnp.zeros((seq - keys, 2 * width), BF)
    total_ref[0:width] = dot_lt(u_ref[...], dqkv_ref[:, 0:width]).astype(BF)
    for part in (1, 2):
        cols = slice(part * width, (part + 1) * width)
        total_ref[cols] = dot_lt(u_ref[0:keys], dqkv_ref[0:keys, cols]).astype(BF)
    share_out(info_ref, total_ref, send_ref, keep_ref)


def attend_back(info, q, k, v, p, mixed, dm, u):
    seq, width = u.shape
    return call(
        attend_back_kernel,
        "attend_back",
        [
            shape((3 * width // 2, width), BF),
            shape((3 * width // 2, width), BF),
            shape((seq, 3 * width), BF),
        ],
        [IN_SMEM] + [IN_VMEM] * 7,
        scratch=[pltpu.VMEM((3 * width, width), BF)],
        flops=11_000_000_000,
        moved=16_000_000,
    )(info, q, k, v, p, mixed, dm, u)


def input_back_kernel(keys, dqkv_ref, da_ref, w_ref, du_ref):
    seq, width = da_ref.shape
    du_ref[0:keys] = (
        da_ref[0:keys].astype(F32) + dot_rt(dqkv_ref[0:keys], w_ref[...])
    ).astype(BF)
    du_ref[keys:seq] = (
        da_ref[keys:seq].astype(F32) + dot_rt(dqkv_ref[keys:seq, :width], w_ref[:, :width])
    ).astype(BF)


def input_back(dqkv, da, w_qkv):
    seq, width = da.shape
    return call(
        functools.partial(input_back_kernel, seq * 3 // 4),
        "input_back",
        shape((seq, width), BF),
        [IN_VMEM] * 3,
        flops=2_500_000_000,
        moved=6_000_000,
    )(dqkv, da, w_qkv)


def stages(count):
    bits = count.bit_length() - 1
    first = (bits - 1) // 3
    one = list(range(bits))
    two = one[first : 2 * first] + one[:first] + one[2 * first :]
    return list(zip(one, two))


def route(count, pair):
    return [
        (place * 2 + core, (place ^ 1 << pair[core]) * 2 + core)
        for place in range(count)
        for core in (0, 1)
    ]


def exchange(block, pair):
    return lax.ppermute(block, ("dp", "section"), route(lax.axis_size("dp"), pair))


def across(block):
    return lax.ppermute(block, "section", [(0, 1), (1, 0)])


def combine_kernel(stage, extra, bits_ref, keep_ref, come_ref, *outs):
    rows = keep_ref.shape[0] - extra
    if len(outs) == 1:
        outs[0][...] = (keep_ref[...].astype(F32) + come_ref[...].astype(F32)).astype(BF)
        return
    send_ref, next_ref = outs
    half = rows // 2
    mine = bits_ref[stage] * half
    for out_ref, start in ((send_ref, half - mine), (next_ref, mine)):
        place = pl.ds(pl.multiple_of(start, TILE), half)
        out_ref[0:half] = (keep_ref[place].astype(F32) + come_ref[place].astype(F32)).astype(BF)
        if extra:
            out_ref[half:] = (
                keep_ref[rows:].astype(F32) + come_ref[rows:].astype(F32)
            ).astype(BF)


def combine(bits, stage, extra, keep, come):
    rows, width = keep.shape
    if stage is None:
        outs = [shape((rows, width), BF)]
    else:
        outs = [shape(((rows - extra) // 2 + extra, width), BF)] * 2
    return call(
        functools.partial(combine_kernel, stage, extra),
        "combine",
        outs,
        [IN_SMEM, IN_VMEM, IN_VMEM],
        limit=8,
        flops=rows * width,
        moved=rows * width * 4,
    )(bits, keep, come)


def merge_kernel(stage, bits_ref, own_ref, come_ref, out_ref):
    rows = own_ref.shape[0]
    mine = bits_ref[stage] * rows
    out_ref[pl.ds(pl.multiple_of(mine, TILE), rows)] = own_ref[...]
    out_ref[pl.ds(pl.multiple_of(rows - mine, TILE), rows)] = come_ref[...]


def merge(bits, stage, own, come):
    rows, width = own.shape
    return call(
        functools.partial(merge_kernel, stage),
        "merge",
        shape((2 * rows, width), BF),
        [IN_SMEM, IN_VMEM, IN_VMEM],
        limit=8,
        moved=rows * width * 8,
    )(bits, own, come)


def reduce_scatter(bits, extra, send, keep):
    come = across(send)
    plan = stages(lax.axis_size("dp"))
    halved = 0
    for stage, pair in enumerate(plan):
        if (keep.shape[0] - extra) % (2 * TILE):
            (keep,) = combine(bits, None, extra, keep, come)
            send = keep
        else:
            send, keep = combine(bits, stage, extra, keep, come)
            halved = stage + 1
        come = exchange(send, pair)
    (keep,) = combine(bits, None, extra, keep, come)
    return keep, halved


def all_gather(bits, halved, block):
    plan = stages(lax.axis_size("dp"))
    for stage in reversed(range(halved)):
        block = merge(bits, stage, block, exchange(block, plan[stage]))
    return block


def body(
    tokens, cotangent, lengths, train_counts,
    w_qkv, w_out, w_up, b_up, w_down, b_down, gain_one, bias_one, gain_two, bias_two,
):
    core = lax.axis_index("section")
    place = lax.axis_index("dp")
    at_first = core == 0
    seq = tokens.shape[0] // lengths.shape[0]
    width = tokens.shape[1]
    hidden = w_up.shape[2]
    plan = stages(lax.axis_size("dp"))
    bits = jnp.stack(
        [jnp.where(at_first, place >> one & 1, place >> two & 1) for one, two in plan]
    ).astype(jnp.int32)
    length = lax.dynamic_index_in_dim(lengths, core, keepdims=True)
    count = lax.dynamic_index_in_dim(train_counts, core, keepdims=True)
    info = jnp.concatenate([core[None].astype(jnp.int32), length])
    info_all = jnp.stack([core.astype(jnp.int32), jnp.int32(seq)])
    vec = jnp.concatenate(
        [
            b_up.reshape(hidden // width, width),
            b_down, gain_one, bias_one, gain_two, bias_two,
            jnp.zeros((1, width), F32),
        ]
    )
    mine = (w_qkv[0], vec, w_out[0], w_up[0], w_down[0])
    other = tuple(across(member) for member in mine)
    layer_one = tuple(jnp.where(at_first, a, b) for a, b in zip(mine, other))
    layer_two = tuple(jnp.where(at_first, b, a) for a, b in zip(mine, other))
    u_one = lax.dynamic_slice_in_dim(tokens, core * seq, seq)
    dy_two = lax.dynamic_slice_in_dim(cotangent, core * seq, seq)

    def forward(u, weights):
        qkv, vec, out, up, down_w = weights
        q, k, v, p, mixed = attend(count, u, qkv)
        x1, s1, h, g, slope, x2, s2, y = feed(vec, u, mixed, out, up, down_w)
        return y, (u, q, k, v, p, mixed, x1, s1, h, g, slope, x2, s2)

    def backward(info, dy, weights, kept):
        qkv, vec, out, up, down_w = weights
        u, q, k, v, p, mixed, x1, s1, h, g, slope, x2, s2 = kept
        send_a, keep_a, dm, da = feed_back(
            info, vec, dy, x2, s2, g, slope, h, x1, s1, mixed, down_w, up, out
        )
        send_b, keep_b, dqkv = attend_back(info, q, k, v, p, mixed, dm, u)
        du = input_back(dqkv, da, qkv)
        part_a, halved_a = reduce_scatter(bits, TILE, send_a, keep_a)
        part_b, halved_b = reduce_scatter(bits, 0, send_b, keep_b)
        rows = part_a.shape[0] - TILE
        small = part_a[rows:]
        part_a = all_gather(bits, halved_a, part_a[:rows])
        part_b = all_gather(bits, halved_b, part_b)
        return du, part_a, part_b, small

    middle, kept_one = forward(u_one, layer_one)
    last, kept_two = forward(middle, layer_two)
    du_two, a_two, b_two, small_two = backward(info, dy_two, layer_two, kept_two)
    du_one, a_one, b_one, small_one = backward(info_all, du_two, layer_one, kept_one)

    def collected(one, two):
        own = jnp.where(at_first, one, two)
        come = across(jnp.where(at_first, two, one))
        top = jnp.where(at_first, own, come)
        bottom = jnp.where(at_first, come, own)
        return jnp.concatenate([top, bottom]).astype(F32)

    feed_grads = collected(a_one, a_two)
    qkv_grads = collected(b_one, b_two)
    small = jnp.where(at_first, small_one, small_two).astype(F32)
    grad_w_down = feed_grads[:hidden]
    grad_w_up = jnp.concatenate(
        [feed_grads[hidden + i * width : hidden + (i + 1) * width] for i in range(hidden // width)],
        axis=1,
    )
    grad_w_out = feed_grads[hidden + hidden // width * width :]
    grad_w_qkv = jnp.concatenate([qkv_grads[i * width : (i + 1) * width] for i in range(3)], axis=1)

    row_mask = jnp.arange(seq)[:, None] < length[0]
    last = jnp.where(row_mask, last, jnp.zeros((), BF))
    half = width // 2

    def placed(block):
        left, right = block[:, :half], block[:, half:]
        come = across(jnp.where(at_first, right, left))
        own = jnp.where(at_first, left, right)
        return jnp.concatenate([jnp.where(at_first, own, come), jnp.where(at_first, come, own)])

    per = hidden // width
    return (
        placed(last),
        placed(du_one),
        grad_w_qkv[None],
        grad_w_out[None],
        grad_w_up[None],
        small[0:per].reshape(1, hidden),
        grad_w_down[None],
        small[per : per + 1],
        small[per + 1 : per + 2],
        small[per + 2 : per + 3],
        small[per + 3 : per + 4],
        small[per + 4 : per + 5],
    )


def solution(mesh):
    matrix = P("section", None, None)
    vector = P("section", None)
    return jax.shard_map(
        body,
        mesh=mesh,
        in_specs=(
            P("dp", None),
            P("dp", None),
            P("dp"),
            P("dp"),
            matrix,
            matrix,
            matrix,
            vector,
            matrix,
            vector,
            vector,
            vector,
            vector,
            vector,
        ),
        out_specs=(
            P("dp", "section"),
            P("dp", "section"),
            matrix,
            matrix,
            matrix,
            vector,
            matrix,
            vector,
            vector,
            vector,
            vector,
            vector,
        ),
        check_vma=False,
    )
```

```python
import functools

import jax
import jax.numpy as jnp
from jax import lax
from jax.experimental import pallas as pl
from jax.experimental.pallas import tpu as pltpu
from jax.sharding import PartitionSpec as P

HEAD_DIM = 128
EPS = 1e-05
LOG2E = 1.4426950408889634
ROOT = 0.7978845608028654
CUBE = 0.044715
BF = jnp.bfloat16
F32 = jnp.float32
TILE = 16
CORE, COUNT, LENGTH, BITS = 0, 1, 2, 3
LANES = 128
MIB = 1 << 20

IN_VMEM = pl.BlockSpec(memory_space=pltpu.VMEM)
IN_SMEM = pl.BlockSpec(memory_space=pltpu.SMEM)
ANYWHERE = pl.BlockSpec(memory_space=pl.ANY)
IN_HBM = pl.BlockSpec(memory_space=pltpu.HBM)
DMA = pltpu.SemaphoreType.DMA


def shape(dims, kind=BF):
    return jax.ShapeDtypeStruct(dims, kind)


def call(kernel, name, operands, outs, scratch=(), limit=24, flops=0, moved=0, after=()):
    count = len(operands)

    def run(*refs):
        kernel(*refs[:count], *refs[count + len(after) :])

    return pl.pallas_call(
        run,
        out_shape=[out for out, _ in outs],
        in_specs=[spec for _, spec in operands] + [ANYWHERE] * len(after),
        out_specs=[spec for _, spec in outs],
        scratch_shapes=list(scratch),
        compiler_params=pltpu.CompilerParams(vmem_limit_bytes=limit * MIB),
        cost_estimate=pl.CostEstimate(flops=flops, bytes_accessed=moved, transcendentals=0),
        name=name,
    )(*[array for array, _ in operands], *after)


def product(left, right, over):
    return lax.dot_general(left, right, (over, ((), ())), preferred_element_type=F32)


def dot(left, right):
    return product(left, right, ((1,), (0,)))


def dot_rt(left, right):
    return product(left, right, ((1,), (1,)))


def dot_lt(left, right):
    return product(left, right, ((0,), (0,)))


def mean(block):
    return jnp.mean(block, axis=1, keepdims=True)


def down(block):
    return jnp.sum(block, axis=0, keepdims=True)


def normed(block):
    centred = block - mean(block)
    scale = lax.rsqrt(mean(centred * centred) + EPS)
    return centred * scale, scale


class Copies:
    def __init__(self, sems):
        self.sems = sems
        self.used = 0

    def start(self, source, target):
        copy = pltpu.make_async_copy(source, target, self.sems.at[self.used])
        self.used += 1
        copy.start()
        return copy

    def choose(self, own, refs, target, cols=None):
        sem = self.sems.at[self.used]
        self.used += 1
        if cols is not None:
            refs = [ref.at[:, cols] for ref in refs]
            target = target.at[:, cols]

        @pl.when(own)
        def _():
            pltpu.make_async_copy(refs[0], target, sem).start()

        @pl.when(jnp.logical_not(own))
        def _():
            pltpu.make_async_copy(refs[1], target, sem).start()

        return pltpu.make_async_copy(refs[0], target, sem)


class Refs:
    def __init__(self, names, refs):
        self.__dict__.update(zip(names, refs, strict=True))


def named(kernel, ins, outs, scratch, name, limit, flops, moved, after=()):
    names = list(ins) + list(outs) + list(scratch)

    def run(*refs):
        kernel(Refs(names, refs))

    results = call(
        run,
        name,
        list(ins.values()),
        list(outs.values()),
        list(scratch.values()),
        limit=limit,
        flops=flops,
        moved=moved,
        after=after,
    )
    return dict(zip(outs, results))


def pairs(weights, *names):
    return {
        f"{name}_{which}": held(array) if which == "own" else (array, ANYWHERE)
        for name in names
        for which, array in zip(("own", "other"), weights[name])
    }


def both(r, name):
    return [getattr(r, name + "_own"), getattr(r, name + "_other")]


def stored(dims, kind=BF):
    return (pltpu.HBM(dims, kind), IN_HBM)


def passed(dims, kind=BF):
    return (shape(dims, kind), IN_VMEM)


def held(array):
    return (pltpu.with_memory_space_constraint(array, pltpu.HBM), IN_HBM)


def near(array):
    return (array, IN_VMEM)


def scalars(array):
    return (array, IN_SMEM)


def head_cols(head):
    return slice(head * HEAD_DIM, (head + 1) * HEAD_DIM)


def attention(copies, count, u, w, waits, q, k, v, inv, mixed, e, e_out):
    seq, width = u.shape
    keys = k.shape[0]
    factor = HEAD_DIM**-0.5 * LOG2E
    places = lax.broadcasted_iota(jnp.int32, (keys, 1), 0)
    bias = jnp.where(places < count, 0.0, -1e30).astype(F32)
    waits[0]()
    k[...] = dot(u[0:keys], w[:, width : 2 * width]).astype(BF)
    waits[1]()
    v[...] = dot(u[0:keys], w[:, 2 * width :]).astype(BF)
    waits[2]()
    q[...] = dot(u[...], w[:, :width]).astype(BF)
    saves = []
    for head in range(width // HEAD_DIM):
        cols = head_cols(head)
        scores = dot_rt(k[:, cols], q[:, cols]) * factor + bias
        powers = jnp.exp2(scores - jnp.max(scores, axis=0, keepdims=True))
        scale = 1.0 / down(powers)
        inv[head : head + 1] = scale
        low = powers.astype(BF)
        e[head] = low
        if e_out is not None:
            saves.append(copies.start(e.at[head], e_out.at[head]))
        mixed[cols] = (dot(v[:, cols].T, low) * scale).astype(BF)
    return saves


def feed(vec, u, mixed, w_out, w_up, w_down, ready, x1_ref, s1_ref, h_ref, g_ref, slope_ref, x2_ref, s2_ref):
    width, hidden = w_up.shape
    ready[0]()
    a = u[...].astype(F32) + dot_lt(mixed[...], w_out[...])
    x1, s1 = normed(a)
    x1_ref[...] = x1.astype(BF)
    s1_ref[...] = s1
    h = x1 * vec[3:4] + vec[4:5]
    h_low = h.astype(BF)
    h_ref[...] = h_low
    f = h + vec[2:3]
    ready[1]()
    ready[2]()
    for part in range(hidden // width):
        cols = slice(part * width, (part + 1) * width)
        z = dot(h_low, w_up[:, cols]) + vec[part : part + 1]
        square = z * z
        curve = jnp.tanh(z * (ROOT + ROOT * CUBE * square))
        gate = 0.5 * curve + 0.5
        g = (z * gate).astype(BF)
        g_ref[:, cols] = g
        slope = gate + (0.5 * z) * (1.0 - curve * curve) * (ROOT + 3 * ROOT * CUBE * square)
        slope_ref[:, cols] = slope.astype(BF)
        f = f + dot(g, w_down[cols])
    x2, s2 = normed(f)
    x2_ref[...] = x2.astype(BF)
    s2_ref[...] = s2
    return x2 * vec[5:6] + vec[6:7]


def feed_back(vec, dy, x2, s2, slope, x1, s1, mixed, inv, w_down, w_up, w_out, ready, df_ref, dz_ref, da_ref, dm_ref, inner_ref, small_ref):
    seq, width = dy.shape
    hidden = w_up.shape[1]
    x2 = x2[...].astype(F32)
    small = [None] * 7
    small[6] = down(dy)
    small[5] = down(dy * x2)
    t = dy * vec[5:6]
    df = s2[...] * (t - mean(t) - x2 * mean(t * x2))
    small[2] = down(df)
    df_low = df.astype(BF)
    df_ref[...] = df_low
    dh = df
    ready[0]()
    for part in range(hidden // width):
        cols = slice(part * width, (part + 1) * width)
        dz = (dot_rt(df_low, w_down[cols]) * slope[:, cols].astype(F32)).astype(BF)
        dz_ref[:, cols] = dz
        small[part] = down(dz.astype(F32))
        dh = dh + dot_rt(dz, w_up[:, cols])
    ready[1]()
    x1 = x1[...].astype(F32)
    small[4] = down(dh)
    small[3] = down(dh * x1)
    t = dh * vec[3:4]
    da = (s1[...] * (t - mean(t) - x1 * mean(t * x1))).astype(BF)
    da_ref[...] = da
    inner_ref[...] = jnp.zeros_like(inner_ref)
    for head in range(width // HEAD_DIM):
        cols = head_cols(head)
        low = (dot_rt(w_out[cols], da) * inv[head : head + 1]).astype(BF)
        inner_ref[head : head + 1] = down(low.astype(F32) * mixed[cols].astype(F32))
        dm_ref[cols] = low
    bottom = jnp.concatenate(small + [jnp.zeros((LANES - 7, width), F32)], axis=0)
    small_ref[...] = bottom.T.astype(BF)


def feed_grads(core, g, df, h, dz, mixed, da, small, send_ref, keep_ref):
    seq, width = df.shape
    hidden = g.shape[1]
    half = width // 2
    for out_ref, begin in ((send_ref, (1 - core) * half), (keep_ref, core * half)):
        begin = pl.multiple_of(begin, half)
        rows = pl.ds(begin, half)
        out_ref[:, 0:hidden] = dot_lt(h[:, rows], dz[...]).astype(BF)
        at = hidden
        out_ref[:, at : at + width] = dot(mixed[rows], da[...]).astype(BF)
        for part in range(hidden // width):
            at += width
            these = pl.ds(pl.multiple_of(begin + part * width, half), half)
            out_ref[:, at : at + width] = dot_lt(g[:, these], df[...]).astype(BF)
        out_ref[:, at + width :] = small[rows]


def first_kernel(r):
    core = r.core[0]
    seq, width = r.u.shape
    copies = Copies(r.sems)
    rows = copies.start(r.tokens.at[pl.ds(pl.multiple_of(core * seq, TILE), seq)], r.u)
    parts = [
        copies.choose(core == 0, both(r, "qkv"), r.w, slice(part * width, (part + 1) * width))
        for part in (1, 2, 0)
    ]

    def begin():
        rows.wait()
        parts[0].wait()

    saves = attention(
        copies, r.core[COUNT], r.u, r.w, [begin, parts[1].wait, parts[2].wait],
        r.q_hold, r.k_hold, r.v_hold, r.inv, r.mixed, r.e_hold, r.e,
    )
    saves += [
        copies.start(getattr(r, name + "_hold"), getattr(r, name)) for name in ("q", "k", "v")
    ]
    for save in saves:
        save.wait()


def attend_first(core, seq, tokens, weights):
    width = tokens.shape[1]
    keys = seq * 3 // 4
    heads = width // HEAD_DIM
    return named(
        first_kernel,
        {"core": scalars(core), "tokens": held(tokens)}
        | pairs(weights, "qkv"),
        {
            "q": stored((seq, width)),
            "k": stored((keys, width)),
            "v": stored((keys, width)),
            "e": stored((heads, keys, seq)),
            "inv": passed((8, seq), F32),
            "mixed": passed((width, seq)),
            "u": passed((seq, width)),
        },
        {
            "w": pltpu.VMEM((width, 3 * width), BF),
            "q_hold": pltpu.VMEM((seq, width), BF),
            "k_hold": pltpu.VMEM((keys, width), BF),
            "v_hold": pltpu.VMEM((keys, width), BF),
            "e_hold": pltpu.VMEM((heads, keys, seq), BF),
            "sems": DMA((16,)),
        },
        "attend_first",
        limit=26,
        flops=160_000_000_000,
        moved=10_000_000,
    )


KEPT = ("x1", "s1", "h", "g", "slope", "x2", "s2")


def middle_kernel(r):
    core = r.core[0]
    seq, width = r.u.shape
    copies = Copies(r.sems)
    own = core == 0
    here = pl.ds(pl.multiple_of(core * seq, TILE), seq)
    ready = [
        copies.choose(own, both(r, "out"), r.w_out),
        copies.choose(own, both(r, "up"), r.w_up),
        copies.choose(own, both(r, "down"), r.w_down),
    ]
    qkv = [
        copies.choose(
            jnp.logical_not(own), both(r, "qkv"), r.w_qkv, slice(part * width, (part + 1) * width)
        )
        for part in (1, 2, 0)
    ]
    ready_two = [
        copies.choose(jnp.logical_not(own), both(r, "out"), r.w_out_two),
        copies.choose(jnp.logical_not(own), both(r, "up"), r.w_up_two),
        copies.choose(jnp.logical_not(own), both(r, "down"), r.w_down_two),
    ]
    incoming = copies.start(r.cotangent.at[here], r.dy)
    saves = [copies.start(r.mixed, r.mixed_out), copies.start(r.inv, r.inv_out)]
    one = jnp.where(own, r.vec_own[...], r.vec_other[...])
    two = jnp.where(own, r.vec_other[...], r.vec_own[...])
    y = feed(
        one, r.u, r.mixed, r.w_out, r.w_up, r.w_down,
        [copy.wait for copy in ready],
        *[getattr(r, "new_" + name) for name in KEPT],
    )
    r.y[...] = y.astype(BF)
    for name in KEPT:
        saves.append(copies.start(getattr(r, "new_" + name), getattr(r, name)))
    early, saves = saves, []
    attention(
        copies, r.core[COUNT], r.y, r.w_qkv, [copy.wait for copy in qkv],
        r.q, r.k, r.v, r.inv_two, r.mixed_two, r.e, None,
    )
    for save in early:
        save.wait()
    y = feed(
        two, r.y, r.mixed_two, r.w_out_two, r.w_up_two, r.w_down_two,
        [copy.wait for copy in ready_two],
        *[getattr(r, "new_" + name) for name in KEPT],
    )
    places = lax.broadcasted_iota(jnp.int32, (seq, 1), 0)
    valid = places < r.core[LENGTH]
    r.last_hold[...] = jnp.where(valid, y, 0.0).astype(BF)
    saves.append(copies.start(r.last_hold, r.last))
    incoming.wait()
    dy = jnp.where(valid, r.dy[...].astype(F32), 0.0)
    nothing = [lambda: None] * 2
    feed_back(
        two, dy, r.new_x2, r.new_s2, r.new_slope, r.new_x1, r.new_s1, r.mixed_two, r.inv_two,
        r.w_down_two, r.w_up_two, r.w_out_two, nothing, r.df, r.dz, r.da, r.dm, r.inner, r.small,
    )
    feed_grads(
        core, r.new_g, r.df, r.new_h, r.dz, r.mixed_two, r.da, r.small, r.send, r.keep
    )
    for save in saves:
        save.wait()


def middle(core, cotangent, vecs, first, weights):
    seq, width = first["u"].shape
    keys = seq * 3 // 4
    heads = width // HEAD_DIM
    hidden = weights["up"][0].shape[1]
    wide, narrow, tall = (seq, hidden), (seq, width), (seq, 1)
    kept = {
        "x1": (narrow, BF), "s1": (tall, F32), "h": (narrow, BF), "g": (wide, BF),
        "slope": (wide, BF), "x2": (narrow, BF), "s2": (tall, F32),
    }
    grads = (width // 2, 2 * hidden + width + LANES)
    return named(
        middle_kernel,
        {
            "core": scalars(core),
            "cotangent": held(cotangent),
            "vec_own": (vecs[0], IN_VMEM),
            "vec_other": (vecs[1], IN_VMEM),
            "mixed": near(first["mixed"]),
            "inv": near(first["inv"]),
            "u": near(first["u"]),
        }
        | pairs(weights, "qkv", "out", "up", "down"),
        {name: stored(*what) for name, what in kept.items()}
        | {
            "mixed_out": stored((width, seq)),
            "inv_out": stored((8, seq), F32),
            "last": stored(narrow),
            "y": passed(narrow),
            "q": passed(narrow),
            "k": passed((keys, width)),
            "v": passed((keys, width)),
            "e": passed((heads, keys, seq)),
            "da": passed(narrow),
            "dm": passed((width, seq)),
            "inner": passed((8, seq), F32),
            "send": passed(grads),
            "keep": passed(grads),
        },
        {f"new_{name}": pltpu.VMEM(*what) for name, what in kept.items()}
        | {
            "dy": pltpu.VMEM(narrow, BF),
            "last_hold": pltpu.VMEM(narrow, BF),
            "inv_two": pltpu.VMEM((8, seq), F32),
            "mixed_two": pltpu.VMEM((width, seq), BF),
            "df": pltpu.VMEM(narrow, BF),
            "dz": pltpu.VMEM(wide, BF),
            "small": pltpu.VMEM((width, LANES), BF),
            "w_qkv": pltpu.VMEM((width, 3 * width), BF),
        }
        | {
            f"w_{name}{end}": pltpu.VMEM(weights[name][0].shape, BF)
            for name in ("out", "up", "down")
            for end in ("", "_two")
        }
        | {"sems": DMA((32,))},
        "middle",
        limit=32,
        flops=600_000_000_000,
        moved=60_000_000,
    )


def bring(r, copies, names):
    return [copies.start(getattr(r, name + "_far"), getattr(r, name + "_near")) for name in names]


def far(arrays):
    return {name + "_far": held(array) for name, array in arrays.items()}


def brought(arrays):
    return {name + "_near": passed(array.shape, array.dtype) for name, array in arrays.items()}


def attend_back_kernel(coming, r):
    core = r.core[0]
    seq, width = r.u.shape
    keys = r.k.shape[0]
    scale = HEAD_DIM**-0.5
    copies = Copies(r.sems)
    going = bring(r, copies, coming)
    own = core == 0
    if coming:
        for name in ("down", "up", "out"):
            going.append(copies.choose(own, both(r, name), getattr(r, "w_" + name)))
        going.append(copies.choose(jnp.logical_not(own), both(r, "qkv"), r.w_qkv))
    else:
        going.append(copies.choose(own, both(r, "qkv"), r.w_qkv))
    for head in range(width // HEAD_DIM):
        cols = head_cols(head)
        at = head * HEAD_DIM
        change = dot(r.v[:, cols], r.dm[cols]) - r.inner[head : head + 1]
        powers = r.e[head]
        ds = (powers.astype(F32) * change).astype(BF)
        dv = dot(powers, r.dm[cols].T)
        r.dqkv[0:keys, 2 * width + at : 2 * width + at + HEAD_DIM] = dv.astype(BF)
        dq = dot(r.k[:, cols].T, ds) * scale
        dk = dot(ds, r.q[:, cols]) * scale
        r.dqkv[:, cols] = dq.T.astype(BF)
        r.dqkv[0:keys, width + at : width + at + HEAD_DIM] = dk.astype(BF)
    half = width // 2
    for out_ref, begin in ((r.send, (1 - core) * half), (r.keep, core * half)):
        rows = pl.ds(pl.multiple_of(begin, half), half)
        out_ref[:, 0:width] = dot_lt(r.u[:, rows], r.dqkv[:, 0:width]).astype(BF)
        out_ref[:, width:] = dot_lt(r.u[0:keys, rows], r.dqkv[0:keys, width:]).astype(BF)
    for copy in going:
        copy.wait()


def attend_back(core, kept, dm, inner, weights, coming, after=()):
    seq, width = kept["q"].shape
    grads = (width // 2, 3 * width)
    more = ("qkv", "down", "up", "out") if coming else ("qkv",)
    return named(
        functools.partial(attend_back_kernel, tuple(coming)),
        {"core": scalars(core)}
        | {name: near(kept[name]) for name in ("q", "k", "v", "e", "u")}
        | {"dm": near(dm), "inner": near(inner)}
        | far(coming)
        | pairs(weights, *more),
        {"send": passed(grads), "keep": passed(grads), "dqkv": passed((seq, 3 * width))}
        | brought(coming)
        | {f"w_{name}": passed(weights[name][0].shape) for name in more},
        {"sems": DMA((16,))},
        "attend_back",
        limit=14,
        flops=220_000_000_000,
        moved=16_000_000,
        after=after,
    )


def input_gradient(dqkv, da, w, keys):
    seq, width = da.shape
    yield slice(0, keys), da[0:keys].astype(F32) + dot_rt(dqkv[0:keys], w[...])
    yield (
        slice(keys, seq),
        da[keys:seq].astype(F32) + dot_rt(dqkv[keys:seq, :width], w[:, :width]),
    )


BACK = ("x2", "s2", "slope", "x1", "s1", "mixed", "inv")


def turn_kernel(coming, r):
    own = r.core[0] == 0
    copies = Copies(r.sems)
    going = bring(r, copies, coming)
    vec = jnp.where(own, r.vec_own[...], r.vec_other[...])
    for rows, values in input_gradient(r.dqkv, r.da_in, r.w_qkv, r.dqkv.shape[0] * 3 // 4):
        r.dy[rows] = values.astype(BF)
    feed_back(
        vec, r.dy[...].astype(F32), r.x2, r.s2, r.slope, r.x1, r.s1, r.mixed, r.inv,
        r.w_down, r.w_up, r.w_out, [lambda: None] * 2, r.df, r.dz, r.da, r.dm, r.inner, r.small,
    )
    for copy in going:
        copy.wait()


def turn(core, vecs, back, da, coming, after=()):
    seq, width = da.shape
    hidden = back["w_up"].shape[1]
    wide, narrow = (seq, hidden), (seq, width)
    return named(
        functools.partial(turn_kernel, tuple(coming)),
        {
            "core": scalars(core),
            "vec_own": (vecs[0], IN_VMEM),
            "vec_other": (vecs[1], IN_VMEM),
            "dqkv": near(back["dqkv"]),
            "da_in": near(da),
        }
        | {name: near(back[name + "_near"]) for name in BACK}
        | {f"w_{name}": near(back["w_" + name]) for name in ("qkv", "down", "up", "out")}
        | far(coming),
        {
            "df": passed(narrow),
            "dz": passed(wide),
            "da": passed(narrow),
            "dm": passed((width, seq)),
            "inner": passed((8, seq), F32),
            "small": passed((width, LANES)),
        }
        | brought(coming),
        {"dy": pltpu.VMEM(narrow, BF), "sems": DMA((16,))},
        "turn",
        limit=24,
        flops=180_000_000_000,
        moved=16_000_000,
        after=after,
    )


def grads_kernel(coming, r):
    core = r.core[0]
    copies = Copies(r.sems)
    going = bring(r, copies, coming)
    seq = r.u.shape[0]
    here = pl.ds(pl.multiple_of(core * seq, TILE), seq)
    going.append(copies.start(r.tokens.at[here], r.u))
    feed_grads(core, r.g, r.df, r.h, r.dz, r.mixed, r.da, r.small, r.send, r.keep)
    for copy in going:
        copy.wait()


def first_grads(core, tokens, back, coming, after=()):
    seq, width = back["df"].shape
    hidden = back["dz"].shape[1]
    grads = (width // 2, 2 * hidden + width + LANES)
    return named(
        functools.partial(grads_kernel, tuple(coming)),
        {"core": scalars(core), "tokens": held(tokens)}
        | {name: near(back[name + "_near"]) for name in ("h", "mixed", "g")}
        | {name: near(back[name]) for name in ("df", "dz", "da", "small")}
        | far(coming),
        {"send": passed(grads), "keep": passed(grads), "u": passed((seq, width))}
        | brought(coming),
        {"sems": DMA((16,))},
        "first_grads",
        limit=14,
        flops=120_000_000_000,
        moved=10_000_000,
        after=after,
    )


def last_kernel(r):
    for rows, values in input_gradient(r.dqkv, r.da, r.w_qkv, r.dqkv.shape[0] * 3 // 4):
        r.du[rows] = values.astype(BF)


def input_back(core, back, da, after=()):
    return named(
        last_kernel,
        {"dqkv": near(back["dqkv"]), "da": near(da), "w_qkv": near(back["w_qkv"])},
        {"du": (shape(da.shape), IN_VMEM)},
        {},
        "input_back",
        limit=12,
        flops=50_000_000_000,
        moved=6_000_000,
        after=after,
    )["du"]


def stages(count):
    bits = count.bit_length() - 1
    first = (bits - 1) // 3
    one = list(range(bits))
    two = one[first : 2 * first] + one[:first] + one[2 * first :]
    return list(zip(one, two))


def exchange(block, bits):
    count = lax.axis_size("dp")
    route = [
        (place * 2 + core, (place ^ 1 << bits[core]) * 2 + core)
        for place in range(count)
        for core in (0, 1)
    ]
    return lax.ppermute(block, ("dp", "section"), route)


def across(block):
    return lax.ppermute(block, "section", [(0, 1), (1, 0)])


def combine_kernel(stage, bits_ref, keep_ref, come_ref, *outs):
    if stage is None:
        outs[0][...] = (keep_ref[...].astype(F32) + come_ref[...].astype(F32)).astype(BF)
        return
    half = keep_ref.shape[0] // 2
    mine = bits_ref[BITS + stage] * half
    for out_ref, start in zip(outs, (half - mine, mine)):
        place = pl.ds(pl.multiple_of(start, TILE), half)
        out_ref[...] = (keep_ref[place].astype(F32) + come_ref[place].astype(F32)).astype(BF)


def combine(bits, stage, keep, come, after=()):
    rows, width = keep.shape
    outs = [shape((rows, width))] if stage is None else [shape((rows // 2, width))] * 2
    return call(
        functools.partial(combine_kernel, stage),
        "combine",
        [scalars(bits), (keep, IN_VMEM), (come, IN_VMEM)],
        [(out, IN_VMEM) for out in outs],
        limit=8,
        flops=rows * width,
        moved=rows * width * 4,
        after=after,
    )


def finish_kernel(*refs):
    out_ref = refs[-1]
    at = 0
    for keep_ref, come_ref in zip(refs[:-1:2], refs[1:-1:2]):
        width = keep_ref.shape[1]
        out_ref[:, at : at + width] = (
            keep_ref[...].astype(F32) + come_ref[...].astype(F32)
        ).astype(BF)
        at += width


def merge_kernel(stage, bits_ref, own_ref, come_ref, out_ref):
    rows = own_ref.shape[0]
    mine = bits_ref[BITS + stage] * rows
    out_ref[pl.ds(pl.multiple_of(mine, TILE), rows)] = own_ref[...]
    out_ref[pl.ds(pl.multiple_of(rows - mine, TILE), rows)] = come_ref[...]


def merge(bits, stage, own, come, after=()):
    rows, width = own.shape
    return call(
        functools.partial(merge_kernel, stage),
        "merge",
        [scalars(bits), (own, IN_VMEM), (come, IN_VMEM)],
        [(shape((2 * rows, width)), IN_VMEM)],
        limit=8,
        moved=rows * width * 8,
        after=after,
    )[0]


class Scatter:
    def __init__(self, bits, arrays):
        self.bits = bits
        self.plan = stages(lax.axis_size("dp"))
        self.keep = arrays["keep"]
        self.come = across(arrays["send"])
        self.stage = 0
        self.halved = 0

    def step(self, after=()):
        if self.keep.shape[0] % (2 * TILE):
            (self.keep,) = combine(self.bits, None, self.keep, self.come, after)
            send = self.keep
        else:
            send, self.keep = combine(self.bits, self.stage, self.keep, self.come, after)
            self.halved = self.stage + 1
        self.come = exchange(send, self.plan[self.stage])
        self.stage += 1
        return (send,)


class Gather:
    def __init__(self, sums, after=()):
        rows = sums[0].keep.shape[0]
        width = sum(member.keep.shape[1] for member in sums)
        pieces = [(array, IN_VMEM) for member in sums for array in (member.keep, member.come)]
        (self.block,) = call(
            finish_kernel,
            "finish",
            pieces,
            [(shape((rows, width)), IN_VMEM)],
            limit=8,
            flops=rows * width,
            moved=rows * width * 4,
            after=after,
        )
        self.bits = sums[0].bits
        self.plan = sums[0].plan
        self.stage = sums[0].halved
        self.begin()

    def begin(self):
        self.stage -= 1
        if self.stage >= 0:
            self.come = exchange(self.block, self.plan[self.stage])

    def step(self, after=()):
        self.block = merge(self.bits, self.stage, self.block, self.come, after)
        self.begin()
        return (self.block,)


def collect_kernel(skip, core_ref, *refs):
    (one_ref, two_ref, one_come_ref, two_come_ref), outs = refs[:4], refs[4:]
    half = one_ref.shape[0]
    core = core_ref[0]

    def write(ref, first, begin):
        rows = slice(begin, begin + half)

        def part(at, width):
            return ref[:, first + at : first + at + width].astype(F32)

        if len(outs) == 1:
            outs[0][0, rows] = part(0, outs[0].shape[2])
            return
        up_ref, out_ref, down_ref, b_up_ref = outs[:4]
        hidden = up_ref.shape[2]
        narrow = out_ref.shape[2]
        count = hidden // narrow
        up_ref[0, rows] = part(0, hidden)
        at = hidden
        out_ref[0, rows] = part(at, narrow)
        for place in range(count):
            at += narrow
            down_ref[0, place * narrow + begin : place * narrow + begin + half] = part(at, narrow)
        small = part(at + narrow, LANES).T
        for place in range(count):
            b_up_ref[:, place * narrow + begin : place * narrow + begin + half] = small[
                place : place + 1
            ]
        for place, ref_out in enumerate(outs[4:]):
            ref_out[:, rows] = small[count + place : count + place + 1]

    @pl.when(core == 0)
    def _():
        write(one_ref, 0, 0)
        write(one_come_ref, 0, half)

    @pl.when(core == 1)
    def _():
        write(two_ref, skip, half)
        write(two_come_ref, skip, 0)


def collect(core, one, two, one_come, two_come, skip, outs, name, after=()):
    half, width = one.shape
    return call(
        functools.partial(collect_kernel, skip),
        name,
        [scalars(core)] + [(array, IN_VMEM) for array in (one, two, one_come, two_come)],
        [(out, IN_VMEM) for out in outs],
        limit=32,
        moved=half * width * 12,
        after=after,
    )


def pack_kernel(r):
    copies = Copies(r.sems)
    names = ("b_up", "b_down", "g1", "c1", "g2", "c2")
    going = [copies.start(getattr(r, name), getattr(r, name + "_hold")) for name in names]
    for copy in going:
        copy.wait()
    width = r.b_down.shape[1]
    parts = r.b_up.shape[1] // width
    r.out[...] = jnp.zeros_like(r.out)
    for part in range(parts):
        r.out[part : part + 1] = r.b_up_hold[:, part * width : (part + 1) * width]
    for place, name in enumerate(names[1:]):
        r.out[parts + place : parts + place + 1] = getattr(r, name + "_hold")[...]


def pack(b_up, b_down, g1, c1, g2, c2):
    arrays = {"b_up": b_up, "b_down": b_down, "g1": g1, "c1": c1, "g2": g2, "c2": c2}
    return named(
        pack_kernel,
        {name: held(array) for name, array in arrays.items()},
        {"out": (shape((8, b_down.shape[1]), F32), IN_VMEM)},
        {name + "_hold": pltpu.VMEM(array.shape, F32) for name, array in arrays.items()}
        | {"sems": DMA((6,))},
        "pack",
        limit=4,
        flops=0,
        moved=20_000,
    )["out"]


def body(
    tokens, cotangent, lengths, train_counts,
    w_qkv, w_out, w_up, b_up, w_down, b_down, gain_one, bias_one, gain_two, bias_two,
):
    index = lax.axis_index("section")
    place = lax.axis_index("dp")
    at_first = index == 0
    seq = tokens.shape[0] // lengths.shape[0]
    width = tokens.shape[1]
    hidden = w_up.shape[2]
    plan = stages(lax.axis_size("dp"))
    first_bit = jnp.array([one for one, _ in plan], jnp.int32)
    other_bit = jnp.array([two for _, two in plan], jnp.int32)
    core = bits = jnp.concatenate(
        [
            index[None].astype(jnp.int32),
            lax.dynamic_slice_in_dim(train_counts, index, 1),
            lax.dynamic_slice_in_dim(lengths, index, 1),
            place >> jnp.where(at_first, first_bit, other_bit) & 1,
        ]
    )
    weights = {
        name: (array[0], across(array[0]))
        for name, array in (("qkv", w_qkv), ("out", w_out), ("up", w_up), ("down", w_down))
    }
    vec = pack(b_up, b_down, gain_one, bias_one, gain_two, bias_two)
    vecs = (vec, across(vec))

    first = attend_first(core, seq, tokens, weights)
    kept = middle(core, cotangent, vecs, first, weights)
    kept["u"] = kept["y"]
    kept_one = {name: kept[name] for name in KEPT} | {
        "mixed": kept["mixed_out"], "inv": kept["inv_out"],
        "q": first["q"], "k": first["k"], "v": first["v"], "e": first["e"],
    }

    def some(*names):
        return {name: kept_one[name] for name in names}

    a_two = Scatter(bits, kept)
    two = attend_back(core, kept, kept["dm"], kept["inner"], weights, some(*BACK), (kept["send"],))
    b_two = Scatter(bits, two)
    mark = a_two.step((two["send"],))
    back = turn(core, vecs, two, kept["da"], some("h", "g"), mark)
    back["mixed_near"] = two["mixed_near"]
    mark = b_two.step((back["df"],))
    mark = a_two.step(mark)
    grads = first_grads(core, tokens, back, some("q", "k", "v", "e"), mark)
    a_one = Scatter(bits, grads)
    mark = b_two.step((grads["send"],))
    mark = a_two.step(mark)
    near_one = {name: grads[name + "_near"] for name in ("q", "k", "v", "e")} | {"u": grads["u"]}
    one = attend_back(
        core, near_one, back["dm"], back["inner"], weights, {}, mark + (grads["send"],)
    )
    b_one = Scatter(bits, one)
    mark = a_one.step((one["send"],))
    mark = a_two.step(mark)
    mark = b_two.step(mark)
    du = input_back(core, one, back["da"], mark)
    mark = b_one.step((du,))
    mark = b_two.step(mark)
    mark = a_one.step(mark)
    all_two = Gather([a_two, b_two], mark)
    mark = b_one.step((all_two.block,))
    mark = a_one.step(mark)
    mark = all_two.step(mark)
    mark = b_one.step(mark)
    mark = a_one.step(mark)
    mark = all_two.step(mark)
    mark = b_one.step(mark)
    feed_one = Gather([a_one], mark)
    mark = all_two.step((feed_one.block,))
    qkv_one = Gather([b_one], mark)
    mark = feed_one.step((qkv_one.block,))
    mark = qkv_one.step(mark)
    mark = all_two.step(mark)
    mark = feed_one.step(mark)
    mark = qkv_one.step(mark)
    mark = feed_one.step(mark)
    mark = qkv_one.step(mark)
    mark = feed_one.step(mark)
    two_come = lax.ppermute(all_two.block, "section", [(0, 1)])
    one_come = lax.ppermute(feed_one.block, "section", [(1, 0)])
    vectors = [shape((1, hidden), F32)] + [shape((1, width), F32)] * 5
    grad_w_up, grad_w_out, grad_w_down, *grad_vectors = collect(
        core,
        feed_one.block,
        all_two.block,
        one_come,
        two_come,
        0,
        [
            shape((1, width, hidden), F32),
            shape((1, width, width), F32),
            shape((1, hidden, width), F32),
        ]
        + vectors,
        "collect_feed",
        mark,
    )
    mark = qkv_one.step((grad_w_out,))
    one_come = lax.ppermute(qkv_one.block, "section", [(1, 0)])
    (grad_w_qkv,) = collect(
        core,
        qkv_one.block,
        all_two.block,
        one_come,
        two_come,
        feed_one.block.shape[1],
        [shape((1, width, 3 * width), F32)],
        "collect_qkv",
    )
    half = width // 2

    def placed(block):
        left, right = block[:, :half], block[:, half:]
        come = across(jnp.where(at_first, right, left))
        own = jnp.where(at_first, left, right)
        return jnp.concatenate([jnp.where(at_first, own, come), jnp.where(at_first, come, own)])

    grad_b_up, grad_b_down, *grad_norms = grad_vectors
    return (
        placed(kept["last"]),
        placed(du),
        grad_w_qkv,
        grad_w_out,
        grad_w_up,
        grad_b_up,
        grad_w_down,
        grad_b_down,
        *grad_norms,
    )


def solution(mesh):
    matrix = P("section", None, None)
    vector = P("section", None)
    weights = (matrix, matrix, matrix, vector, matrix, vector, vector, vector, vector, vector)
    rows = P("dp", None)
    halves = P("dp", "section")
    return jax.shard_map(
        body,
        mesh=mesh,
        in_specs=(rows, rows, P("dp"), P("dp")) + weights,
        out_specs=(halves, halves) + weights,
        check_vma=False,
    )
```

```python
import functools

import jax
import jax.numpy as jnp
from jax import lax
from jax.experimental import pallas as pl
from jax.experimental.pallas import tpu as pltpu
from jax.sharding import PartitionSpec as P

HEAD_DIM = 128
EPS = 1e-05
LOG2E = 1.4426950408889634
ROOT = 0.7978845608028654
CUBE = 0.044715
BF = jnp.bfloat16
DP, SECTION = "dp", "section"
F32 = jnp.float32
TILE = 16
STEP = 8_000_000_000
CORE, BITS = 0, 1
LANES = 128
MIB = 1 << 20

IN_VMEM = pl.BlockSpec(memory_space=pltpu.VMEM)
IN_SMEM = pl.BlockSpec(memory_space=pltpu.SMEM)
ANYWHERE = pl.BlockSpec(memory_space=pl.ANY)
IN_HBM = pl.BlockSpec(memory_space=pltpu.HBM)
DMA = pltpu.SemaphoreType.DMA


def shape(dims, kind=BF):
    return jax.ShapeDtypeStruct(dims, kind)


def call(kernel, name, operands, outs, scratch=(), limit=24, flops=0, moved=0, after=()):
    count = len(operands)

    def run(*refs):
        kernel(*refs[:count], *refs[count + len(after) :])

    return pl.pallas_call(
        run,
        out_shape=[out for out, _ in outs],
        in_specs=[spec for _, spec in operands] + [ANYWHERE] * len(after),
        out_specs=[spec for _, spec in outs],
        scratch_shapes=list(scratch),
        compiler_params=pltpu.CompilerParams(vmem_limit_bytes=limit * MIB),
        cost_estimate=pl.CostEstimate(flops=flops, bytes_accessed=moved, transcendentals=0),
        name=name,
    )(*[array for array, _ in operands], *after)


def product(left, right, over):
    return lax.dot_general(left, right, (over, ((), ())), preferred_element_type=F32)


def dot(left, right):
    return product(left, right, ((1,), (0,)))


def dot_rt(left, right):
    return product(left, right, ((1,), (1,)))


def dot_lt(left, right):
    return product(left, right, ((0,), (0,)))


def mean(block):
    return jnp.mean(block, axis=1, keepdims=True)


def down(block):
    return jnp.sum(block, axis=0, keepdims=True)


def normed(block):
    centred = block - mean(block)
    scale = lax.rsqrt(mean(centred * centred) + EPS)
    return centred * scale, scale


class Copies:
    def __init__(self, sm):
        self.sm = sm
        self.used = 0

    def start(self, source, target):
        copy = pltpu.make_async_copy(source, target, self.sm.at[self.used])
        self.used += 1
        copy.start()
        return copy

    def choose(self, own, refs, target, cols=None):
        sem = self.sm.at[self.used]
        self.used += 1
        if cols is not None:
            refs = [ref.at[:, cols] for ref in refs]
            target = target.at[:, cols]

        @pl.when(own)
        def _():
            pltpu.make_async_copy(refs[0], target, sem).start()

        @pl.when(jnp.logical_not(own))
        def _():
            pltpu.make_async_copy(refs[1], target, sem).start()

        return pltpu.make_async_copy(refs[0], target, sem)


class Refs:
    def __init__(self, names, refs):
        self.__dict__.update(zip(names, refs, strict=True))


def named(kernel, ins, outs, scratch, name, limit, flops, moved, after=()):
    names = list(ins) + list(outs) + list(scratch)

    def run(*refs):
        kernel(Refs(names, refs))

    results = call(
        run,
        name,
        list(ins.values()),
        list(outs.values()),
        list(scratch.values()),
        limit=limit,
        flops=flops,
        moved=moved,
        after=after,
    )
    return dict(zip(outs, results))


def pairs(weights, *names):
    return {
        f"{name}_{which}": held(array) if which == "own" else (array, ANYWHERE)
        for name in names
        for which, array in zip(("own", "other"), weights[name])
    }


def both(r, name):
    return [getattr(r, name + "_own"), getattr(r, name + "_other")]


def stored(dims, kind=BF):
    return (pltpu.HBM(dims, kind), IN_HBM)


def passed(dims, kind=BF):
    return (shape(dims, kind), IN_VMEM)


def held(array):
    return (pltpu.with_memory_space_constraint(array, pltpu.HBM), IN_HBM)


def near(array):
    return (array, IN_VMEM)


def scalars(array):
    return (array, IN_SMEM)


def head_cols(head):
    return slice(head * HEAD_DIM, (head + 1) * HEAD_DIM)


def attention(copies, count, u, w, waits, q, k, v, inv, mixed, e, e_out, early=lambda: []):
    seq, width = u.shape
    keys = k.shape[0]
    factor = HEAD_DIM**-0.5 * LOG2E
    waits[0]()
    k[...] = dot(u[0:keys], w[:, width : 2 * width]).astype(BF)
    waits[1]()
    v[...] = dot(u[0:keys], w[:, 2 * width :]).astype(BF)
    waits[2]()
    q[...] = dot(u[...], w[:, :width]).astype(BF)
    saves = early()
    places = lax.broadcasted_iota(jnp.int32, (keys, 1), 0)
    bias = jnp.where(places < count(), 0.0, -1e30).astype(F32)
    for head in range(width // HEAD_DIM):
        cols = head_cols(head)
        scores = dot_rt(k[:, cols], q[:, cols]) * factor + bias
        powers = jnp.exp2(scores - jnp.max(scores, axis=0, keepdims=True))
        scale = 1.0 / down(powers)
        inv[head : head + 1] = scale
        low = powers.astype(BF)
        e[head] = low
        if e_out is not None:
            saves.append(copies.start(e.at[head], e_out.at[head]))
        mixed[cols] = (dot(v[:, cols].T, low) * scale).astype(BF)
    return saves


def feed(vec, u, mixed, w_out, w_up, w_down, ready, x1_ref, s1_ref, h_ref, g_ref, slope_ref, x2_ref, s2_ref):
    width, hidden = w_up.shape
    ready[0]()
    a = u[...].astype(F32) + dot_lt(mixed[...], w_out[...])
    x1, s1 = normed(a)
    x1_ref[...] = x1.astype(BF)
    s1_ref[...] = s1
    h = x1 * vec[3:4] + vec[4:5]
    h_low = h.astype(BF)
    h_ref[...] = h_low
    f = h + vec[2:3]
    ready[1]()
    ready[2]()
    for part in range(hidden // width):
        cols = slice(part * width, (part + 1) * width)
        z = (dot(h_low, w_up[:, cols]) + vec[part : part + 1]).astype(BF)
        square = z * z
        curve = jnp.tanh(z * (ROOT + ROOT * CUBE * square))
        gate = 0.5 * curve + 0.5
        g = z * gate
        g_ref[:, cols] = g
        steep = (0.5 * z) * (1.0 - curve * curve) * (ROOT + 3 * ROOT * CUBE * square)
        slope_ref[:, cols] = gate + steep
        f = f + dot(g, w_down[cols])
    x2, s2 = normed(f)
    x2_ref[...] = x2.astype(BF)
    s2_ref[...] = s2
    return x2 * vec[5:6] + vec[6:7]


def feed_back(vec, dy, x2, s2, sl, x1, s1, mixed, inv, w_down, w_up, w_out, ready, df_ref, dz_ref, da_ref, dm_ref, inner_ref, small_ref):
    seq, width = dy.shape
    hidden = w_up.shape[1]
    x2 = x2[...].astype(F32)
    small = [None] * 7
    small[6] = down(dy)
    small[5] = down(dy * x2)
    t = dy * vec[5:6]
    df = s2[...] * (t - mean(t) - x2 * mean(t * x2))
    small[2] = down(df)
    df_low = df.astype(BF)
    df_ref[...] = df_low
    dh = df
    ready[0]()
    for part in range(hidden // width):
        cols = slice(part * width, (part + 1) * width)
        dz = (dot_rt(df_low, w_down[cols]) * sl[:, cols].astype(F32)).astype(BF)
        dz_ref[:, cols] = dz
        small[part] = down(dz.astype(F32))
        dh = dh + dot_rt(dz, w_up[:, cols])
    ready[1]()
    x1 = x1[...].astype(F32)
    small[4] = down(dh)
    small[3] = down(dh * x1)
    t = dh * vec[3:4]
    da = (s1[...] * (t - mean(t) - x1 * mean(t * x1))).astype(BF)
    da_ref[...] = da
    inner_ref[...] = jnp.zeros_like(inner_ref)
    for head in range(width // HEAD_DIM):
        cols = head_cols(head)
        low = (dot_rt(w_out[cols], da) * inv[head : head + 1]).astype(BF)
        inner_ref[head : head + 1] = down(low.astype(F32) * mixed[cols].astype(F32))
        dm_ref[cols] = low
    bottom = jnp.concatenate(small + [jnp.zeros((LANES - 7, width), F32)], axis=0)
    small_ref[...] = bottom.T.astype(BF)


def feed_grads(core, g, df, h, dz, mixed, da, small, send_ref, keep_ref):
    seq, width = df.shape
    hidden = g.shape[1]
    half = width // 2
    for out_ref, begin in ((send_ref, (1 - core) * half), (keep_ref, core * half)):
        begin = pl.multiple_of(begin, half)
        rows = pl.ds(begin, half)
        out_ref[:, 0:hidden] = dot_lt(h[:, rows], dz[...]).astype(BF)
        at = hidden
        out_ref[:, at : at + width] = dot(mixed[rows], da[...]).astype(BF)
        for part in range(hidden // width):
            at += width
            these = pl.ds(pl.multiple_of(begin + part * width, half), half)
            out_ref[:, at : at + width] = dot_lt(g[:, these], df[...]).astype(BF)
        out_ref[:, at + width :] = small[rows]


def first_kernel(r):
    core = r.core[0]
    seq, width = r.u.shape
    copies = Copies(r.sm)
    rows = copies.start(r.tokens.at[pl.ds(pl.multiple_of(core * seq, TILE), seq)], r.u)
    parts = [
        copies.choose(core == 0, both(r, "qkv"), r.w, slice(part * width, (part + 1) * width))
        for part in (1, 2, 0)
    ]

    def begin():
        rows.wait()
        parts[0].wait()

    counting = copies.start(r.counts, r.cn)

    def count():
        counting.wait()
        return r.cn[core]

    saves = attention(
        copies, count, r.u, r.w, [begin, parts[1].wait, parts[2].wait],
        r.q_hold, r.k_hold, r.v_hold, r.inv, r.mixed, r.e_hold, r.e,
        lambda: [
            copies.start(getattr(r, name + "_hold"), getattr(r, name)) for name in ("q", "k", "v")
        ],
    )
    for save in saves:
        save.wait()


def attend_first(core, seq, counts, tokens, weights):
    width = tokens.shape[1]
    keys = seq * 3 // 4
    heads = width // HEAD_DIM
    return named(
        first_kernel,
        {"core": scalars(core), "counts": held(counts), "tokens": held(tokens)}
        | pairs(weights, "qkv"),
        {
            "q": stored((seq, width)),
            "k": stored((keys, width)),
            "v": stored((keys, width)),
            "e": stored((heads, keys, seq)),
            "inv": passed((8, seq), F32),
            "mixed": passed((width, seq)),
            "u": passed((seq, width)),
        },
        {
            "w": pltpu.VMEM((width, 3 * width), BF),
            "q_hold": pltpu.VMEM((seq, width), BF),
            "k_hold": pltpu.VMEM((keys, width), BF),
            "v_hold": pltpu.VMEM((keys, width), BF),
            "e_hold": pltpu.VMEM((heads, keys, seq), BF),
            "cn": pltpu.SMEM(counts.shape, jnp.int32),
            "sm": DMA((16,)),
        },
        "first",
        limit=26,
        flops=160_000_000_000,
        moved=10_000_000,
    )


A2, B2, A1, B1, HEADS, TURN, GRADS, EARLY, LATE, INPUT, OUT, IN = range(12)
PLANS = {A2: (2, True), B2: (3, False), A1: (3, True), B1: (3, False)}
ORDER = (
    HEADS, A2, TURN, A2, B2, GRADS, A2, EARLY, A1, B2, A2, LATE, A1, B2,
    INPUT, B1, A1, A2, B2, A1, B1, A2, OUT, B1, B2, IN, A1, B1,
    A2, A1, B2, B1, A1, B1, B2, A1, B1, B2, B1,
)
KEPT = ("x1", "s1", "h", "g", "sl", "x2", "s2")


def middle_kernel(r):
    core = r.core[0]
    seq, width = r.u.shape
    copies = Copies(r.sm)
    own = core == 0
    here = pl.ds(pl.multiple_of(core * seq, TILE), seq)
    ready = [
        copies.choose(own, both(r, "out"), r.w_out),
        copies.choose(own, both(r, "up"), r.w_up),
        copies.choose(own, both(r, "down"), r.w_down),
    ]
    qkv = [
        copies.choose(
            jnp.logical_not(own), both(r, "qkv"), r.wq, slice(part * width, (part + 1) * width)
        )
        for part in (1, 2, 0)
    ]
    ready_two = [
        copies.choose(jnp.logical_not(own), both(r, "out"), r.w_out_two),
        copies.choose(jnp.logical_not(own), both(r, "up"), r.w_up_two),
        copies.choose(jnp.logical_not(own), both(r, "down"), r.w_down_two),
    ]
    counting = copies.start(r.counts, r.cn)
    measuring = copies.start(r.lengths, r.ln)
    incoming = copies.start(r.ct.at[here], r.dy)
    saves = [copies.start(r.mixed, r.mo), copies.start(r.inv, r.io)]
    one = jnp.where(own, r.va[...], r.vb[...])
    two = jnp.where(own, r.vb[...], r.va[...])
    y = feed(
        one, r.u, r.mixed, r.w_out, r.w_up, r.w_down,
        [copy.wait for copy in ready],
        *[getattr(r, "new_" + name) for name in KEPT],
    )
    r.y[...] = y.astype(BF)
    for name in KEPT:
        saves.append(copies.start(getattr(r, "new_" + name), getattr(r, name)))
    early, saves = saves, []
    counting.wait()
    attention(
        copies, lambda: r.cn[core], r.y, r.wq, [copy.wait for copy in qkv],
        r.q, r.k, r.v, r.inv_two, r.mixed_two, r.e, None,
    )
    for save in early:
        save.wait()
    y = feed(
        two, r.y, r.mixed_two, r.w_out_two, r.w_up_two, r.w_down_two,
        [copy.wait for copy in ready_two],
        *[getattr(r, "new_" + name) for name in KEPT],
    )
    places = lax.broadcasted_iota(jnp.int32, (seq, 1), 0)
    measuring.wait()
    valid = places < r.ln[core]
    r.last[...] = jnp.where(valid, y, 0.0).astype(BF)
    half = width // 2
    for out_ref, begin in ((r.ls, (1 - core) * half), (r.lk, core * half)):
        out_ref[...] = r.last[:, pl.ds(pl.multiple_of(begin, half), half)]
    incoming.wait()
    dy = jnp.where(valid, r.dy[...].astype(F32), 0.0)
    nothing = [lambda: None] * 2
    feed_back(
        two, dy, r.new_x2, r.new_s2, r.new_sl, r.new_x1, r.new_s1, r.mixed_two, r.inv_two,
        r.w_down_two, r.w_up_two, r.w_out_two, nothing, r.df, r.dz, r.da, r.dm, r.ir, r.small,
    )
    feed_grads(
        core, r.new_g, r.df, r.new_h, r.dz, r.mixed_two, r.da, r.small, r.sd, r.kp
    )
    for save in saves:
        save.wait()


def middle(core, counts, lengths, cotangent, vecs, first, weights):
    seq, width = first["u"].shape
    keys = seq * 3 // 4
    heads = width // HEAD_DIM
    hidden = weights["up"][0].shape[1]
    wide, narrow, tall = (seq, hidden), (seq, width), (seq, 1)
    kept = {
        "x1": (narrow, BF), "s1": (tall, F32), "h": (narrow, BF), "g": (wide, BF),
        "sl": (wide, BF), "x2": (narrow, BF), "s2": (tall, F32),
    }
    grads = (width // 2, 2 * hidden + width + LANES)
    return named(
        middle_kernel,
        {
            "core": scalars(core),
            "counts": held(counts),
            "lengths": held(lengths),
            "ct": held(cotangent),
            "va": (vecs[0], IN_VMEM),
            "vb": (vecs[1], IN_VMEM),
            "mixed": near(first["mixed"]),
            "inv": near(first["inv"]),
            "u": near(first["u"]),
        }
        | pairs(weights, "qkv", "out", "up", "down"),
        {name: stored(*what) for name, what in kept.items()}
        | {
            "mo": stored((width, seq)),
            "io": stored((8, seq), F32),
            "ls": passed((seq, width // 2)),
            "lk": passed((seq, width // 2)),
            "y": passed(narrow),
            "q": passed(narrow),
            "k": passed((keys, width)),
            "v": passed((keys, width)),
            "e": passed((heads, keys, seq)),
            "da": passed(narrow),
            "dm": passed((width, seq)),
            "ir": passed((8, seq), F32),
            "sd": passed(grads),
            "kp": passed(grads),
        },
        {f"new_{name}": pltpu.VMEM(*what) for name, what in kept.items()}
        | {
            "dy": pltpu.VMEM(narrow, BF),
            "last": pltpu.VMEM(narrow, BF),
            "cn": pltpu.SMEM(counts.shape, jnp.int32),
            "ln": pltpu.SMEM(lengths.shape, jnp.int32),
            "inv_two": pltpu.VMEM((8, seq), F32),
            "mixed_two": pltpu.VMEM((width, seq), BF),
            "df": pltpu.VMEM(narrow, BF),
            "dz": pltpu.VMEM(wide, BF),
            "small": pltpu.VMEM((width, LANES), BF),
            "wq": pltpu.VMEM((width, 3 * width), BF),
        }
        | {
            f"w_{name}{end}": pltpu.VMEM(weights[name][0].shape, BF)
            for name in ("out", "up", "down")
            for end in ("", "_two")
        }
        | {"sm": DMA((32,))},
        "middle",
        limit=32,
        flops=600_000_000_000,
        moved=60_000_000,
    )


def bring(r, copies, names):
    return [copies.start(getattr(r, name + "_far"), getattr(r, name + "_near")) for name in names]


def far(arrays):
    return {name + "_far": held(array) for name, array in arrays.items()}


def brought(arrays):
    return {name + "_near": passed(array.shape, array.dtype) for name, array in arrays.items()}


def head_back(r, head, powers, out_q, out_k, out_v):
    cols = head_cols(head)
    scale = HEAD_DIM**-0.5
    change = dot(r.v[:, cols], r.dm[cols]) - r.ir[head : head + 1]
    ds = (powers[...].astype(F32) * change).astype(BF)
    out_v[...] = dot(powers[...], r.dm[cols].T).astype(BF)
    out_q[...] = (dot(r.k[:, cols].T, ds) * scale).T.astype(BF)
    out_k[...] = (dot(ds, r.q[:, cols]) * scale).astype(BF)


def early_heads_kernel(r):
    core = r.core[0]
    seq = r.dm.shape[1]
    count = r.dq.shape[1] // HEAD_DIM
    copies = Copies(r.sm)
    loads = {"v": copies.start(r.v_far, r.v), 0: copies.start(r.e_far.at[0], r.e.at[0])}
    loads["k"] = copies.start(r.k_far, r.k)
    loads["q"] = copies.start(r.q_far, r.q)
    for head in range(1, count):
        loads[head] = copies.start(r.e_far.at[head], r.e.at[head])
    here = pl.ds(pl.multiple_of(core * seq, TILE), seq)
    going = [
        copies.start(r.e_far.at[count : 2 * count], r.er),
        copies.start(r.u_far.at[here], r.u),
    ]
    for name in ("v", 0, "k", "q"):
        loads.pop(name).wait()
    for head in range(count):
        cols = head_cols(head)
        if head in loads:
            loads.pop(head).wait()
        head_back(r, head, r.e.at[head], r.dq.at[:, cols], r.dk.at[:, cols], r.dv.at[:, cols])
    for copy in going:
        copy.wait()


def early_heads(core, kept, dm, ir, tokens, after=()):
    seq, width = kept["q"].shape
    keys = kept["k"].shape[0]
    count = width // HEAD_DIM // 2
    arrays = {"q": (seq, width), "k": (keys, width), "v": (keys, width)}
    results = named(
        early_heads_kernel,
        {"core": scalars(core), "u_far": held(tokens)}
        | {name + "_far": held(kept[name]) for name in (*arrays, "e")}
        | {"dm": near(dm), "ir": near(ir)},
        {
            "dq": passed((seq, width // 2)),
            "dk": passed((keys, width // 2)),
            "dv": passed((keys, width // 2)),
            "er": passed((count, keys, seq)),
            "u": passed((seq, width)),
        }
        | {name: passed(dims) for name, dims in arrays.items()},
        {"e": pltpu.VMEM((count, keys, seq), BF), "sm": DMA((16,))},
        "early",
        limit=20,
        flops=110_000_000_000,
        moved=16_000_000,
        after=after,
    )
    return results | {"dm": dm, "ir": ir}


def late_heads_kernel(layer, r):
    core = r.core[0]
    seq, width = r.u.shape
    keys = r.k.shape[0]
    half = width // 2
    heads = width // HEAD_DIM
    copies = Copies(r.sm)
    going = copies.choose(core == layer, both(r, "qkv"), r.wq)
    r.dqkv[:, 0:half] = r.dq[...]
    r.dqkv[0:keys, width : width + half] = r.dk[...]
    r.dqkv[0:keys, 2 * width : 2 * width + half] = r.dv[...]
    for head in range(heads // 2, heads):
        cols = [
            slice(part * width + head * HEAD_DIM, part * width + (head + 1) * HEAD_DIM)
            for part in range(3)
        ]
        head_back(
            r, head, r.er.at[head - heads // 2],
            r.dqkv.at[:, cols[0]], r.dqkv.at[0:keys, cols[1]], r.dqkv.at[0:keys, cols[2]],
        )
    for out_ref, begin in ((r.sd, (1 - core) * half), (r.kp, core * half)):
        rows = pl.ds(pl.multiple_of(begin, half), half)
        out_ref[:, 0:width] = dot_lt(r.u[:, rows], r.dqkv[:, 0:width]).astype(BF)
        out_ref[:, width:] = dot_lt(r.u[0:keys, rows], r.dqkv[0:keys, width:]).astype(BF)
    going.wait()


def late_heads(layer, core, early, weights, after=()):
    seq, width = early["q"].shape
    grads = (width // 2, 3 * width)
    return named(
        functools.partial(late_heads_kernel, layer),
        {"core": scalars(core)}
        | {
            name: near(early[name])
            for name in ("q", "k", "v", "u", "er", "dq", "dk", "dv", "dm", "ir")
        }
        | pairs(weights, "qkv"),
        {
            "sd": passed(grads),
            "kp": passed(grads),
            "dqkv": passed((seq, 3 * width)),
            "wq": passed(weights["qkv"][0].shape),
        },
        {"sm": DMA((1,))},
        "late",
        limit=14,
        flops=110_000_000_000,
        moved=16_000_000,
        after=after,
    )


def heads_kernel(layer, r):
    core = r.core[0]
    seq, width = r.u.shape
    keys = r.k.shape[0]
    copies = Copies(r.sm)
    going = copies.choose(core == layer, both(r, "qkv"), r.wq)
    for head in range(width // HEAD_DIM):
        cols = [
            slice(part * width + head * HEAD_DIM, part * width + (head + 1) * HEAD_DIM)
            for part in range(3)
        ]
        head_back(
            r, head, r.e.at[head],
            r.dqkv.at[:, cols[0]], r.dqkv.at[0:keys, cols[1]], r.dqkv.at[0:keys, cols[2]],
        )
    half = width // 2
    for out_ref, begin in ((r.sd, (1 - core) * half), (r.kp, core * half)):
        rows = pl.ds(pl.multiple_of(begin, half), half)
        out_ref[:, 0:width] = dot_lt(r.u[:, rows], r.dqkv[:, 0:width]).astype(BF)
        out_ref[:, width:] = dot_lt(r.u[0:keys, rows], r.dqkv[0:keys, width:]).astype(BF)
    going.wait()


def all_heads(layer, core, kept, dm, ir, weights, after=()):
    seq, width = kept["q"].shape
    grads = (width // 2, 3 * width)
    return named(
        functools.partial(heads_kernel, layer),
        {"core": scalars(core)}
        | {name: near(kept[name]) for name in ("q", "k", "v", "u", "e")}
        | {"dm": near(dm), "ir": near(ir)}
        | pairs(weights, "qkv"),
        {
            "sd": passed(grads),
            "kp": passed(grads),
            "dqkv": passed((seq, 3 * width)),
            "wq": passed(weights["qkv"][0].shape),
        },
        {"sm": DMA((1,))},
        "heads",
        limit=14,
        flops=220_000_000_000,
        moved=16_000_000,
        after=after,
    )


def input_gradient(dqkv, da, w, keys):
    seq, width = da.shape
    yield slice(0, keys), da[0:keys].astype(F32) + dot_rt(dqkv[0:keys], w[...])
    yield (
        slice(keys, seq),
        da[keys:seq].astype(F32) + dot_rt(dqkv[keys:seq, :width], w[:, :width]),
    )


BACK = ("x2", "s2", "sl", "x1", "s1", "mixed", "inv")


def turn_kernel(coming, r):
    own = r.core[0] == 0
    copies = Copies(r.sm)
    loads = {}
    for name in BACK:
        if name == "sl":
            loads["down"] = copies.choose(own, both(r, "down"), r.w_down)
        loads[name] = copies.start(getattr(r, name + "_in"), getattr(r, name))
        if name == "sl":
            loads["up"] = copies.choose(own, both(r, "up"), r.w_up)
    loads["out"] = copies.choose(own, both(r, "out"), r.w_out)
    going = bring(r, copies, coming)
    vec = jnp.where(own, r.va[...], r.vb[...])
    for rows, values in input_gradient(r.dqkv, r.da_in, r.wq, r.dqkv.shape[0] * 3 // 4):
        r.dy[rows] = values.astype(BF)

    def ready(*names):
        for name in names:
            loads.pop(name).wait()

    ready("x2", "s2")
    feed_back(
        vec, r.dy[...].astype(F32), r.x2, r.s2, r.sl, r.x1, r.s1, r.mixed, r.inv,
        r.w_down, r.w_up, r.w_out, [lambda: ready("down", "sl", "up"), lambda: ready(*list(loads))],
        r.df, r.dz, r.da, r.dm, r.ir, r.small,
    )
    for copy in going:
        copy.wait()


def turn(core, vecs, back, da, kept, weights, coming, after=()):
    seq, width = da.shape
    hidden = weights["up"][0].shape[1]
    wide, narrow = (seq, hidden), (seq, width)
    return named(
        functools.partial(turn_kernel, tuple(coming)),
        {
            "core": scalars(core),
            "va": (vecs[0], IN_VMEM),
            "vb": (vecs[1], IN_VMEM),
            "dqkv": near(back["dqkv"]),
            "da_in": near(da),
            "wq": near(back["wq"]),
        }
        | {name + "_in": held(kept[name]) for name in BACK}
        | pairs(weights, "down", "up", "out")
        | far(coming),
        {
            "df": passed(narrow),
            "dz": passed(wide),
            "da": passed(narrow),
            "dm": passed((width, seq)),
            "ir": passed((8, seq), F32),
            "small": passed((width, LANES)),
        }
        | brought(coming),
        {name: pltpu.VMEM(kept[name].shape, kept[name].dtype) for name in BACK}
        | {f"w_{name}": pltpu.VMEM(weights[name][0].shape, BF) for name in ("down", "up", "out")}
        | {"dy": pltpu.VMEM(narrow, BF), "sm": DMA((24,))},
        "turn",
        limit=36,
        flops=180_000_000_000,
        moved=16_000_000,
        after=after,
    )


def grads_kernel(r):
    feed_grads(
        r.core[0], r.g, r.df, r.h, r.dz, r.mixed, r.da, r.small, r.sd, r.kp
    )


def first_grads(core, back, after=()):
    seq, width = back["df"].shape
    hidden = back["dz"].shape[1]
    grads = (width // 2, 2 * hidden + width + LANES)
    return named(
        grads_kernel,
        {"core": scalars(core)}
        | {name: near(back[name + "_near"]) for name in ("h", "mixed", "g")}
        | {name: near(back[name]) for name in ("df", "dz", "da", "small")},
        {"sd": passed(grads), "kp": passed(grads)},
        {},
        "grads",
        limit=14,
        flops=120_000_000_000,
        moved=10_000_000,
        after=after,
    )


def last_kernel(r):
    seq, width = r.da.shape
    keys = seq * 3 // 4
    half = width // 2
    core = r.core[0]
    for out_ref, begin in ((r.sd, (1 - core) * half), (r.kp, core * half)):
        cols = pl.ds(pl.multiple_of(begin, half), half)
        out_ref[0:keys] = (
            r.da[0:keys, cols].astype(F32) + dot_rt(r.dqkv[0:keys], r.wq[cols])
        ).astype(BF)
        out_ref[keys:seq] = (
            r.da[keys:seq, cols].astype(F32)
            + dot_rt(r.dqkv[keys:seq, :width], r.wq[cols, :width])
        ).astype(BF)


def input_back(core, back, da, after=()):
    return named(
        last_kernel,
        {
            "core": scalars(core),
            "dqkv": near(back["dqkv"]),
            "da": near(da),
            "wq": near(back["wq"]),
        },
        {name: passed((da.shape[0], da.shape[1] // 2)) for name in ("sd", "kp")},
        {},
        "input",
        limit=8,
        flops=50_000_000_000,
        moved=6_000_000,
        after=after,
    )


def stages(count):
    bits = count.bit_length() - 1
    first = (bits - 1) // 3
    one = list(range(bits))
    two = one[first : 2 * first] + one[:first] + one[2 * first :]
    return list(zip(one, two))


def exchange(block, bits):
    count = lax.axis_size(DP)
    route = [
        (place * 2 + core, (place ^ 1 << bits[core]) * 2 + core)
        for place in range(count)
        for core in (0, 1)
    ]
    return lax.ppermute(block, (DP, SECTION), route)


def across(block):
    return lax.ppermute(block, SECTION, [(0, 1), (1, 0)])


def combine_kernel(stage, bits_ref, keep_ref, come_ref, *outs):
    if stage is None:
        outs[0][...] = (keep_ref[...].astype(F32) + come_ref[...].astype(F32)).astype(BF)
        return
    half = keep_ref.shape[0] // 2
    mine = bits_ref[stage] * half
    for out_ref, start in zip(outs, (half - mine, mine)):
        place = pl.ds(pl.multiple_of(start, TILE), half)
        out_ref[...] = (keep_ref[place].astype(F32) + come_ref[place].astype(F32)).astype(BF)


def combine(bits, stage, kp, come, after=()):
    rows, width = kp.shape
    outs = [shape((rows, width))] if stage is None else [shape((rows // 2, width))] * 2
    return call(
        functools.partial(combine_kernel, stage),
        "combine",
        [scalars(bits), (kp, IN_VMEM), (come, IN_VMEM)],
        [(out, IN_VMEM) for out in outs],
        limit=8,
        flops=STEP,
        after=after,
    )


def finish_kernel(*refs):
    out_ref = refs[-1]
    at = 0
    for keep_ref, come_ref in zip(refs[:-1:2], refs[1:-1:2]):
        width = keep_ref.shape[1]
        out_ref[:, at : at + width] = (
            keep_ref[...].astype(F32) + come_ref[...].astype(F32)
        ).astype(BF)
        at += width


def merge_kernel(stage, bits_ref, own_ref, come_ref, out_ref):
    rows = own_ref.shape[0]
    mine = bits_ref[stage] * rows
    out_ref[pl.ds(pl.multiple_of(mine, TILE), rows)] = own_ref[...]
    out_ref[pl.ds(pl.multiple_of(rows - mine, TILE), rows)] = come_ref[...]


def merge(bits, stage, own, come, after=()):
    rows, width = own.shape
    return call(
        functools.partial(merge_kernel, stage),
        "merge",
        [scalars(bits), (own, IN_VMEM), (come, IN_VMEM)],
        [(shape((2 * rows, width)), IN_VMEM)],
        limit=8,
        flops=STEP,
        after=after,
    )[0]


class Sums:
    def __init__(self, bits, arrays, halvings, turned):
        self.bits = bits
        self.turned = turned
        self.plan = stages(lax.axis_size(DP))
        if turned:
            first = (len(self.plan) - 1) // 3
            self.plan = (
                self.plan[first : 2 * first] + self.plan[:first] + self.plan[2 * first :]
            )
        self.halvings = halvings
        self.block = arrays["kp"]
        self.come = across(arrays["sd"])
        self.stage = 0
        self.halved = []
        self.doubling = False

    def place(self, stage):
        count = len(self.plan)
        first = (count - 1) // 3
        if self.turned and stage < 2 * first:
            stage = (stage + first) % (2 * first)
        return BITS + stage

    def left(self):
        return self.come is not None

    def step(self, after=()):
        if self.doubling:
            self.block = merge(self.bits, self.place(self.halved.pop()), self.block, self.come, after)
            return self.double()
        if self.stage == len(self.plan):
            (self.block,) = combine(self.bits, None, self.block, self.come, after)
            self.doubling = True
            return self.double()
        if self.stage >= self.halvings or self.block.shape[0] % (2 * TILE):
            (self.block,) = combine(self.bits, None, self.block, self.come, after)
            sd = self.block
        else:
            place = self.place(self.stage)
            sd, self.block = combine(self.bits, place, self.block, self.come, after)
            self.halved.append(self.stage)
        self.come = exchange(sd, self.plan[self.stage])
        self.stage += 1
        return (sd,)

    def double(self):
        self.come = exchange(self.block, self.plan[self.halved[-1]]) if self.halved else None
        return (self.block,)


def place_kernel(core_ref, keep_ref, come_ref, out_ref, mark_ref):
    rows = keep_ref.shape[0]
    mark_ref[...] = jnp.zeros_like(mark_ref)

    @pl.when(core_ref[0] == 0)
    def _():
        out_ref[0:rows] = keep_ref[...]
        out_ref[rows:] = come_ref[...]

    @pl.when(core_ref[0] == 1)
    def _():
        out_ref[0:rows] = come_ref[...]
        out_ref[rows:] = keep_ref[...]


def place_halves(core, kp, come, after=()):
    rows, width = kp.shape
    return call(
        place_kernel,
        "place",
        [scalars(core), (kp, IN_VMEM), (come, IN_VMEM)],
        [(shape((2 * rows, width)), IN_VMEM), (shape((8, LANES), F32), IN_VMEM)],
        limit=8,
        flops=STEP,
        after=after,
    )


def collect_kernel(count, mine, parts, r):
    half = r.one.shape[0]

    def write(ref, begin):
        copies = Copies(r.sm)
        going = []
        at = 0
        for name, offset, width in parts:
            cols = slice(at, at + width)
            r.hold[:, cols] = ref[:, cols].astype(F32)
            target = getattr(r, name).at[0, offset + begin : offset + begin + half]
            going.append(copies.start(r.hold.at[:, cols], target))
            at += width
        for copy in going:
            copy.wait()

    def vectors(own_ref, come_ref, begin):
        at = sum(width for _, _, width in parts)
        for ref, place in ((own_ref, begin), (come_ref, half - begin)):
            small = ref[:, at:].astype(F32).T
            for row in range(count):
                width = r.out.shape[2]
                r.b_up[:, row * width + place : row * width + place + half] = small[row : row + 1]
            for row, name in enumerate(("bd", "g1", "c1", "g2", "c2")):
                getattr(r, name)[:, place : place + half] = small[count + row : count + row + 1]

    @pl.when(r.core[0] == 0)
    def _():
        if count:
            vectors(r.one_own, r.one, 0)
        write(r.one, 0 if mine else half)

    @pl.when(r.core[0] == 1)
    def _():
        if count:
            vectors(r.two_own, r.two, half)
        write(r.two, half if mine else 0)


def collect(core, one, two, outs, parts, name, after=(), begun=None, own=None, small=None):
    half = one.shape[0]
    begun = begun or {}
    ins = {"core": scalars(core), "one": (one, IN_VMEM), "two": (two, IN_VMEM)}
    if small:
        ins |= {"one_own": (own[0], IN_VMEM), "two_own": (own[1], IN_VMEM)}
    ins |= {name + "_begun": (array, ANYWHERE) for name, array in begun.items()}
    results = {name: (shape(dims, F32), ANYWHERE) for name, dims in outs.items()}
    results |= {name: (shape(dims, F32), IN_VMEM) for name, dims in (small or {}).items()}
    scratch = {
        "hold": pltpu.VMEM((half, sum(width for _, _, width in parts)), F32),
        "sm": DMA((len(parts),)),
    }
    names = list(ins) + list(results) + list(scratch)
    count = len(ins)
    first = count - len(begun)
    rows = small["b_up"][1] // small["bd"][1] if small else 0

    def run(*refs):
        collect_kernel(rows, not begun, parts, Refs(names, refs[:count] + refs[count + len(after) :]))

    values = pl.pallas_call(
        run,
        out_shape=[out for out, _ in results.values()],
        in_specs=[spec for _, spec in ins.values()] + [ANYWHERE] * len(after),
        out_specs=[spec for _, spec in results.values()],
        scratch_shapes=list(scratch.values()),
        input_output_aliases={first + place: place for place in range(len(begun))},
        compiler_params=pltpu.CompilerParams(vmem_limit_bytes=16 * MIB),
        cost_estimate=pl.CostEstimate(flops=STEP, bytes_accessed=0, transcendentals=0),
        name=name,
    )(*[array for array, _ in ins.values()], *after)
    return dict(zip(results, values))


def pack_kernel(r):
    copies = Copies(r.sm)
    names = ("b_up", "bd", "g1", "c1", "g2", "c2")
    going = [copies.start(getattr(r, name), getattr(r, name + "_hold")) for name in names]
    for copy in going:
        copy.wait()
    width = r.bd.shape[1]
    parts = r.b_up.shape[1] // width
    r.out[...] = jnp.zeros_like(r.out)
    for part in range(parts):
        r.out[part : part + 1] = r.b_up_hold[:, part * width : (part + 1) * width]
    for place, name in enumerate(names[1:]):
        r.out[parts + place : parts + place + 1] = getattr(r, name + "_hold")[...]


def pack(b_up, bd, g1, c1, g2, c2):
    arrays = {"b_up": b_up, "bd": bd, "g1": g1, "c1": c1, "g2": g2, "c2": c2}
    return named(
        pack_kernel,
        {name: held(array) for name, array in arrays.items()},
        {"out": (shape((8, bd.shape[1]), F32), IN_VMEM)},
        {name + "_hold": pltpu.VMEM(array.shape, F32) for name, array in arrays.items()}
        | {"sm": DMA((6,))},
        "pack",
        limit=4,
        flops=0,
        moved=20_000,
    )["out"]


def body(
    tokens, cotangent, lengths, train_counts,
    wq, w_out, w_up, b_up, w_down, bd, gain_one, bias_one, gain_two, bias_two,
):
    index = lax.axis_index(SECTION)
    place = lax.axis_index(DP)
    at_first = index == 0
    seq = tokens.shape[0] // lengths.shape[0]
    width = tokens.shape[1]
    hidden = w_up.shape[2]
    plan = stages(lax.axis_size(DP))
    first_bit = jnp.array([one for one, _ in plan], jnp.int32)
    other_bit = jnp.array([two for _, two in plan], jnp.int32)
    core = bits = jnp.concatenate(
        [
            index[None].astype(jnp.int32),
            place >> jnp.where(at_first, first_bit, other_bit) & 1,
        ]
    )
    weights = {"qkv": (wq[0], across(wq[0]))}
    vec = pack(b_up, bd, gain_one, bias_one, gain_two, bias_two)
    later = lax.optimization_barrier((w_out[0], w_up[0], w_down[0], vec))[:3]
    weights |= {name: (array, across(array)) for name, array in zip(("out", "up", "down"), later)}
    vecs = (vec, across(vec))

    first = attend_first(core, seq, train_counts, tokens, weights)
    kept = middle(core, train_counts, lengths, cotangent, vecs, first, weights)
    kept["u"] = kept["y"]
    kept_one = {name: kept[name] for name in KEPT} | {
        "mixed": kept["mo"], "inv": kept["io"],
        "q": first["q"], "k": first["k"], "v": first["v"], "e": first["e"],
    }

    def some(*names):
        return {name: kept_one[name] for name in names}

    sums = {A2: Sums(bits, kept, *PLANS[A2])}
    last_come = across(kept["ls"])
    mark = (kept["sd"],)
    for name in ORDER:
        if name == HEADS:
            two = all_heads(1, core, kept, kept["dm"], kept["ir"], weights, mark)
            sums[B2] = Sums(bits, two, *PLANS[B2])
            mark = (two["sd"],)
        elif name == TURN:
            back = turn(
                core, vecs, two, kept["da"], kept_one, weights, some("h", "g", "mixed"), mark
            )
            mark = (back["df"],)
        elif name == GRADS:
            grads = first_grads(core, back, mark)
            sums[A1] = Sums(bits, grads, *PLANS[A1])
            mark = (grads["sd"],)
        elif name == EARLY:
            early = early_heads(core, kept_one, back["dm"], back["ir"], tokens, mark)
            mark = (early["dq"],)
        elif name == LATE:
            one = late_heads(0, core, early, weights, mark)
            sums[B1] = Sums(bits, one, *PLANS[B1])
            mark = (one["sd"],)
        elif name == INPUT:
            du = input_back(core, one, back["da"], mark)
            du_come = across(du["sd"])
            mark = (du["sd"],)
        elif name == OUT:
            output, *mark = place_halves(core, kept["lk"], last_come, mark)
        elif name == IN:
            grad_tokens, *mark = place_halves(core, du["kp"], du_come, mark)
        elif sums[name].left():
            mark = sums[name].step(mark)
    for name in sums:
        while sums[name].left():
            mark = sums[name].step(mark)
    a_one, a_two, b_one, b_two = (sums[name].block for name in (A1, A2, B1, B2))
    vectors = {"b_up": (1, hidden)} | {
        name: (1, width) for name in ("bd", "g1", "c1", "g2", "c2")
    }
    feed_outs = {"up": (1, width, hidden), "out": (1, width, width), "down": (1, hidden, width)}
    feed_parts = [("up", 0, hidden), ("out", 0, width)]
    feed_parts += [("down", place * width, width) for place in range(hidden // width)]
    qkv_outs, qkv_parts = {"qkv": (1, width, 3 * width)}, [("qkv", 0, 3 * width)]

    def come(one, two):
        return lax.ppermute(one, SECTION, [(1, 0)]), lax.ppermute(two, SECTION, [(0, 1)])

    feed_come, qkv_come = come(a_one, a_two), come(b_one, b_two)
    feed_begun = collect(core, a_one, a_two, feed_outs, feed_parts, "own", mark)
    qkv_begun = collect(
        core, b_one, b_two, qkv_outs, qkv_parts, "own", mark
    )
    feed_done = collect(
        core, *feed_come, feed_outs, feed_parts, "come", (),
        feed_begun, (a_one, a_two), vectors,
    )
    grad_w_qkv = collect(
        core, *qkv_come, qkv_outs, qkv_parts, "come", (), qkv_begun
    )["qkv"]
    grad_w_up, grad_w_out, grad_w_down, *grad_vectors = feed_done.values()
    grad_b_up, grad_b_down, *grad_norms = grad_vectors
    return (
        output,
        grad_tokens,
        grad_w_qkv,
        grad_w_out,
        grad_w_up,
        grad_b_up,
        grad_w_down,
        grad_b_down,
        *grad_norms,
    )


def solution(mesh):
    matrix = P(SECTION, None, None)
    vector = P(SECTION, None)
    weights = (matrix, matrix, matrix, vector, matrix, vector, vector, vector, vector, vector)
    rows = P(DP, None)
    halves = P(DP, SECTION)
    return jax.shard_map(
        body,
        mesh=mesh,
        in_specs=(rows, rows, P(DP), P(DP)) + weights,
        out_specs=(halves, halves) + weights,
        check_vma=False,
    )
```

```python
import functools

import jax
import jax.numpy as jnp
from jax import lax
from jax.experimental import pallas as pl
from jax.experimental.pallas import tpu as pltpu
from jax.sharding import PartitionSpec as P

HEAD_DIM = 128
EPS = 1e-05
LOG2E = 1.4426950408889634
ROOT = 0.7978845608028654
CUBE = 0.044715
BF = jnp.bfloat16
DP, SECTION = "dp", "section"
F32 = jnp.float32
TILE = 16
STEP = 8_000_000_000
CORE, BITS = 0, 1
LANES = 128
MIB = 1 << 20

IN_VMEM = pl.BlockSpec(memory_space=pltpu.VMEM)
IN_SMEM = pl.BlockSpec(memory_space=pltpu.SMEM)
ANYWHERE = pl.BlockSpec(memory_space=pl.ANY)
IN_HBM = pl.BlockSpec(memory_space=pltpu.HBM)
DMA = pltpu.SemaphoreType.DMA


def shape(dims, kind=BF):
    return jax.ShapeDtypeStruct(dims, kind)


def call(kernel, name, operands, outs, scratch=(), limit=24, flops=0, moved=0, after=()):
    count = len(operands)

    def run(*refs):
        kernel(*refs[:count], *refs[count + len(after) :])

    return pl.pallas_call(
        run,
        out_shape=[out for out, _ in outs],
        in_specs=[spec for _, spec in operands] + [ANYWHERE] * len(after),
        out_specs=[spec for _, spec in outs],
        scratch_shapes=list(scratch),
        compiler_params=pltpu.CompilerParams(vmem_limit_bytes=limit * MIB),
        cost_estimate=pl.CostEstimate(flops=flops, bytes_accessed=moved, transcendentals=0),
        name=name,
    )(*[array for array, _ in operands], *after)


def product(left, right, over):
    return lax.dot_general(left, right, (over, ((), ())), preferred_element_type=F32)


def dot(left, right):
    return product(left, right, ((1,), (0,)))


def dot_rt(left, right):
    return product(left, right, ((1,), (1,)))


def dot_lt(left, right):
    return product(left, right, ((0,), (0,)))


def mean(block):
    return jnp.mean(block, axis=1, keepdims=True)


def down(block):
    return jnp.sum(block, axis=0, keepdims=True)


def normed(block):
    centred = block - mean(block)
    scale = lax.rsqrt(mean(centred * centred) + EPS)
    return centred * scale, scale


class Copies:
    def __init__(self, sm):
        self.sm = sm
        self.used = 0

    def start(self, source, target):
        copy = pltpu.make_async_copy(source, target, self.sm.at[self.used])
        self.used += 1
        copy.start()
        return copy

    def choose(self, own, refs, target, cols=None):
        sem = self.sm.at[self.used]
        self.used += 1
        if cols is not None:
            refs = [ref.at[:, cols] for ref in refs]
            target = target.at[:, cols]

        @pl.when(own)
        def _():
            pltpu.make_async_copy(refs[0], target, sem).start()

        @pl.when(jnp.logical_not(own))
        def _():
            pltpu.make_async_copy(refs[1], target, sem).start()

        return pltpu.make_async_copy(refs[0], target, sem)


class Refs:
    def __init__(self, names, refs):
        self.__dict__.update(zip(names, refs, strict=True))


def named(kernel, ins, outs, scratch, name, limit, flops, moved, after=()):
    names = list(ins) + list(outs) + list(scratch)

    def run(*refs):
        kernel(Refs(names, refs))

    results = call(
        run,
        name,
        list(ins.values()),
        list(outs.values()),
        list(scratch.values()),
        limit=limit,
        flops=flops,
        moved=moved,
        after=after,
    )
    return dict(zip(outs, results))


def pairs(weights, *names):
    return {
        f"{name}_{which}": held(array) if which == "own" else (array, ANYWHERE)
        for name in names
        for which, array in zip(("own", "other"), weights[name])
    }


def both(r, name):
    return [getattr(r, name + "_own"), getattr(r, name + "_other")]


def stored(dims, kind=BF):
    return (pltpu.HBM(dims, kind), IN_HBM)


def passed(dims, kind=BF):
    return (shape(dims, kind), IN_VMEM)


def held(array):
    return (pltpu.with_memory_space_constraint(array, pltpu.HBM), IN_HBM)


def near(array):
    return (array, IN_VMEM)


def scalars(array):
    return (array, IN_SMEM)


def head_cols(head):
    return slice(head * HEAD_DIM, (head + 1) * HEAD_DIM)


def attention(copies, count, u, w, waits, q, k, v, inv, mixed, e, e_out, early=lambda: []):
    seq, width = u.shape
    keys = k.shape[0]
    factor = HEAD_DIM**-0.5 * LOG2E
    waits[0]()
    k[...] = dot(u[0:keys], w[:, width : 2 * width]).astype(BF)
    waits[1]()
    v[...] = dot(u[0:keys], w[:, 2 * width :]).astype(BF)
    waits[2]()
    q[...] = dot(u[...], w[:, :width]).astype(BF)
    saves = early()
    places = lax.broadcasted_iota(jnp.int32, (keys, 1), 0)
    bias = jnp.where(places < count(), 0.0, -1e30).astype(F32)
    for head in range(width // HEAD_DIM):
        cols = head_cols(head)
        scores = dot_rt(k[:, cols], q[:, cols]) * factor + bias
        powers = jnp.exp2(scores - jnp.max(scores, axis=0, keepdims=True))
        scale = 1.0 / down(powers)
        inv[head : head + 1] = scale
        low = powers.astype(BF)
        e[head] = low
        if e_out is not None:
            saves.append(copies.start(e.at[head], e_out.at[head]))
        mixed[cols] = (dot(v[:, cols].T, low) * scale).astype(BF)
    return saves


def feed(vec, u, mixed, w_out, w_up, w_down, ready, x1_ref, s1_ref, h_ref, g_ref, slope_ref, x2_ref, s2_ref):
    width, hidden = w_up.shape
    ready[0]()
    a = u[...].astype(F32) + dot_lt(mixed[...], w_out[...])
    x1, s1 = normed(a)
    x1_ref[...] = x1.astype(BF)
    s1_ref[...] = s1
    h = x1 * vec[3:4] + vec[4:5]
    h_low = h.astype(BF)
    h_ref[...] = h_low
    f = h + vec[2:3]
    ready[1]()
    ready[2]()
    for part in range(hidden // width):
        cols = slice(part * width, (part + 1) * width)
        z = (dot(h_low, w_up[:, cols]) + vec[part : part + 1]).astype(BF)
        square = z * z
        curve = jnp.tanh(z * (ROOT + ROOT * CUBE * square))
        gate = 0.5 * curve + 0.5
        g = z * gate
        g_ref[:, cols] = g
        steep = (0.5 * z) * (1.0 - curve * curve) * (ROOT + 3 * ROOT * CUBE * square)
        slope_ref[:, cols] = gate + steep
        f = f + dot(g, w_down[cols])
    x2, s2 = normed(f)
    x2_ref[...] = x2.astype(BF)
    s2_ref[...] = s2
    return x2 * vec[5:6] + vec[6:7]


def feed_back(vec, dy, x2, s2, sl, x1, s1, mixed, inv, w_down, w_up, w_out, ready, df_ref, dz_ref, da_ref, dm_ref, inner_ref, small_ref):
    seq, width = dy.shape
    hidden = w_up.shape[1]
    x2 = x2[...].astype(F32)
    small = [None] * 7
    small[6] = down(dy)
    small[5] = down(dy * x2)
    t = dy * vec[5:6]
    df = s2[...] * (t - mean(t) - x2 * mean(t * x2))
    small[2] = down(df)
    df_low = df.astype(BF)
    df_ref[...] = df_low
    dh = df
    ready[0]()
    for part in range(hidden // width):
        cols = slice(part * width, (part + 1) * width)
        dz = (dot_rt(df_low, w_down[cols]) * sl[:, cols].astype(F32)).astype(BF)
        dz_ref[:, cols] = dz
        small[part] = down(dz.astype(F32))
        dh = dh + dot_rt(dz, w_up[:, cols])
    ready[1]()
    x1 = x1[...].astype(F32)
    small[4] = down(dh)
    small[3] = down(dh * x1)
    t = dh * vec[3:4]
    da = (s1[...] * (t - mean(t) - x1 * mean(t * x1))).astype(BF)
    da_ref[...] = da
    inner_ref[...] = jnp.zeros_like(inner_ref)
    for head in range(width // HEAD_DIM):
        cols = head_cols(head)
        low = (dot_rt(w_out[cols], da) * inv[head : head + 1]).astype(BF)
        inner_ref[head : head + 1] = down(low.astype(F32) * mixed[cols].astype(F32))
        dm_ref[cols] = low
    bottom = jnp.concatenate(small + [jnp.zeros((LANES - 7, width), F32)], axis=0)
    small_ref[...] = bottom.T.astype(BF)


def feed_grads(core, g, df, h, dz, mixed, da, small, send_ref, keep_ref):
    seq, width = df.shape
    hidden = g.shape[1]
    half = width // 2
    for out_ref, begin in ((send_ref, (1 - core) * half), (keep_ref, core * half)):
        begin = pl.multiple_of(begin, half)
        rows = pl.ds(begin, half)
        out_ref[:, 0:hidden] = dot_lt(h[:, rows], dz[...]).astype(BF)
        at = hidden
        out_ref[:, at : at + width] = dot(mixed[rows], da[...]).astype(BF)
        for part in range(hidden // width):
            at += width
            these = pl.ds(pl.multiple_of(begin + part * width, half), half)
            out_ref[:, at : at + width] = dot_lt(g[:, these], df[...]).astype(BF)
        out_ref[:, at + width :] = small[rows]


def first_kernel(r):
    core = r.core[0]
    seq, width = r.u.shape
    copies = Copies(r.sm)
    rows = copies.start(r.tokens.at[pl.ds(pl.multiple_of(core * seq, TILE), seq)], r.u)
    parts = [
        copies.choose(core == 0, both(r, "qkv"), r.w, slice(part * width, (part + 1) * width))
        for part in (1, 2, 0)
    ]

    def begin():
        rows.wait()
        parts[0].wait()

    counting = copies.start(r.counts, r.cn)

    def count():
        counting.wait()
        return r.cn[core]

    saves = attention(
        copies, count, r.u, r.w, [begin, parts[1].wait, parts[2].wait],
        r.q_hold, r.k_hold, r.v_hold, r.inv, r.mixed, r.e_hold, r.e,
        lambda: [
            copies.start(getattr(r, name + "_hold"), getattr(r, name)) for name in ("q", "k", "v")
        ],
    )
    for save in saves:
        save.wait()


def attend_first(core, seq, counts, tokens, weights):
    width = tokens.shape[1]
    keys = seq * 3 // 4
    heads = width // HEAD_DIM
    return named(
        first_kernel,
        {"core": scalars(core), "counts": held(counts), "tokens": held(tokens)}
        | pairs(weights, "qkv"),
        {
            "q": stored((seq, width)),
            "k": stored((keys, width)),
            "v": stored((keys, width)),
            "e": stored((heads, keys, seq)),
            "inv": passed((8, seq), F32),
            "mixed": passed((width, seq)),
            "u": passed((seq, width)),
        },
        {
            "w": pltpu.VMEM((width, 3 * width), BF),
            "q_hold": pltpu.VMEM((seq, width), BF),
            "k_hold": pltpu.VMEM((keys, width), BF),
            "v_hold": pltpu.VMEM((keys, width), BF),
            "e_hold": pltpu.VMEM((heads, keys, seq), BF),
            "cn": pltpu.SMEM(counts.shape, jnp.int32),
            "sm": DMA((16,)),
        },
        "first",
        limit=26,
        flops=160_000_000_000,
        moved=10_000_000,
    )


A2, B2, A1, B1, HEADS, TURN, GRADS, EARLY, LATE, INPUT, OUT, IN, OWN, COME = range(14)
PLANS = {A2: (3, True), B2: (3, False), A1: (3, True), B1: (3, False)}
ORDER = (
    HEADS, A2, TURN, A2, GRADS, B2, A2, EARLY, A1, B2, A2, LATE, A1, B2,
    A2, INPUT, A1, B1, A2, B2, A1, B1, OUT, A2, B1, B2, IN, A1,
    B1, A2, A1, B2, B1, A1, B1, B2, A1, OWN, B1, B2, COME, B1,
)
KEPT = ("x1", "s1", "h", "g", "sl", "x2", "s2")


def middle_kernel(r):
    core = r.core[0]
    seq, width = r.u.shape
    copies = Copies(r.sm)
    own = core == 0
    here = pl.ds(pl.multiple_of(core * seq, TILE), seq)
    ready = [
        copies.choose(own, both(r, "out"), r.w_out),
        copies.choose(own, both(r, "up"), r.w_up),
        copies.choose(own, both(r, "down"), r.w_down),
    ]
    qkv = [
        copies.choose(
            jnp.logical_not(own), both(r, "qkv"), r.wq, slice(part * width, (part + 1) * width)
        )
        for part in (1, 2, 0)
    ]
    ready_two = [
        copies.choose(jnp.logical_not(own), both(r, "out"), r.w_out_two),
        copies.choose(jnp.logical_not(own), both(r, "up"), r.w_up_two),
        copies.choose(jnp.logical_not(own), both(r, "down"), r.w_down_two),
    ]
    counting = copies.start(r.counts, r.cn)
    measuring = copies.start(r.lengths, r.ln)
    incoming = copies.start(r.ct.at[here], r.dy)
    saves = [copies.start(r.mixed, r.mo), copies.start(r.inv, r.io)]
    one = jnp.where(own, r.va[...], r.vb[...])
    two = jnp.where(own, r.vb[...], r.va[...])
    y = feed(
        one, r.u, r.mixed, r.w_out, r.w_up, r.w_down,
        [copy.wait for copy in ready],
        *[getattr(r, "new_" + name) for name in KEPT],
    )
    r.y[...] = y.astype(BF)
    for name in KEPT:
        saves.append(copies.start(getattr(r, "new_" + name), getattr(r, name)))
    early, saves = saves, []
    counting.wait()
    attention(
        copies, lambda: r.cn[core], r.y, r.wq, [copy.wait for copy in qkv],
        r.q, r.k, r.v, r.inv_two, r.mixed_two, r.e, None,
    )
    for save in early:
        save.wait()
    y = feed(
        two, r.y, r.mixed_two, r.w_out_two, r.w_up_two, r.w_down_two,
        [copy.wait for copy in ready_two],
        *[getattr(r, "new_" + name) for name in KEPT],
    )
    places = lax.broadcasted_iota(jnp.int32, (seq, 1), 0)
    measuring.wait()
    valid = places < r.ln[core]
    r.last[...] = jnp.where(valid, y, 0.0).astype(BF)
    half = width // 2
    for out_ref, begin in ((r.ls, (1 - core) * half), (r.lk, core * half)):
        out_ref[...] = r.last[:, pl.ds(pl.multiple_of(begin, half), half)]
    incoming.wait()
    dy = jnp.where(valid, r.dy[...].astype(F32), 0.0)
    nothing = [lambda: None] * 2
    feed_back(
        two, dy, r.new_x2, r.new_s2, r.new_sl, r.new_x1, r.new_s1, r.mixed_two, r.inv_two,
        r.w_down_two, r.w_up_two, r.w_out_two, nothing, r.df, r.dz, r.da, r.dm, r.ir, r.small,
    )
    feed_grads(
        core, r.new_g, r.df, r.new_h, r.dz, r.mixed_two, r.da, r.small, r.sd, r.kp
    )
    for save in saves:
        save.wait()


def middle(core, counts, lengths, cotangent, vecs, first, weights):
    seq, width = first["u"].shape
    keys = seq * 3 // 4
    heads = width // HEAD_DIM
    hidden = weights["up"][0].shape[1]
    wide, narrow, tall = (seq, hidden), (seq, width), (seq, 1)
    kept = {
        "x1": (narrow, BF), "s1": (tall, F32), "h": (narrow, BF), "g": (wide, BF),
        "sl": (wide, BF), "x2": (narrow, BF), "s2": (tall, F32),
    }
    grads = (width // 2, 2 * hidden + width + LANES)
    return named(
        middle_kernel,
        {
            "core": scalars(core),
            "counts": held(counts),
            "lengths": held(lengths),
            "ct": held(cotangent),
            "va": (vecs[0], IN_VMEM),
            "vb": (vecs[1], IN_VMEM),
            "mixed": near(first["mixed"]),
            "inv": near(first["inv"]),
            "u": near(first["u"]),
        }
        | pairs(weights, "qkv", "out", "up", "down"),
        {name: stored(*what) for name, what in kept.items()}
        | {
            "mo": stored((width, seq)),
            "io": stored((8, seq), F32),
            "ls": passed((seq, width // 2)),
            "lk": passed((seq, width // 2)),
            "y": passed(narrow),
            "q": passed(narrow),
            "k": passed((keys, width)),
            "v": passed((keys, width)),
            "e": passed((heads, keys, seq)),
            "da": passed(narrow),
            "dm": passed((width, seq)),
            "ir": passed((8, seq), F32),
            "sd": passed(grads),
            "kp": passed(grads),
        },
        {f"new_{name}": pltpu.VMEM(*what) for name, what in kept.items()}
        | {
            "dy": pltpu.VMEM(narrow, BF),
            "last": pltpu.VMEM(narrow, BF),
            "cn": pltpu.SMEM(counts.shape, jnp.int32),
            "ln": pltpu.SMEM(lengths.shape, jnp.int32),
            "inv_two": pltpu.VMEM((8, seq), F32),
            "mixed_two": pltpu.VMEM((width, seq), BF),
            "df": pltpu.VMEM(narrow, BF),
            "dz": pltpu.VMEM(wide, BF),
            "small": pltpu.VMEM((width, LANES), BF),
            "wq": pltpu.VMEM((width, 3 * width), BF),
        }
        | {
            f"w_{name}{end}": pltpu.VMEM(weights[name][0].shape, BF)
            for name in ("out", "up", "down")
            for end in ("", "_two")
        }
        | {"sm": DMA((32,))},
        "middle",
        limit=32,
        flops=600_000_000_000,
        moved=60_000_000,
    )


def bring(r, copies, names):
    return [copies.start(getattr(r, name + "_far"), getattr(r, name + "_near")) for name in names]


def far(arrays):
    return {name + "_far": held(array) for name, array in arrays.items()}


def brought(arrays):
    return {name + "_near": passed(array.shape, array.dtype) for name, array in arrays.items()}


def head_back(r, head, powers, out_q, out_k, out_v):
    cols = head_cols(head)
    scale = HEAD_DIM**-0.5
    change = dot(r.v[:, cols], r.dm[cols]) - r.ir[head : head + 1]
    ds = (powers[...].astype(F32) * change).astype(BF)
    out_v[...] = dot(powers[...], r.dm[cols].T).astype(BF)
    out_q[...] = (dot(r.k[:, cols].T, ds) * scale).T.astype(BF)
    out_k[...] = (dot(ds, r.q[:, cols]) * scale).astype(BF)


def early_heads_kernel(r):
    core = r.core[0]
    seq = r.dm.shape[1]
    count = r.dq.shape[1] // HEAD_DIM
    copies = Copies(r.sm)
    loads = {"v": copies.start(r.v_far, r.v), 0: copies.start(r.e_far.at[0], r.e.at[0])}
    loads["k"] = copies.start(r.k_far, r.k)
    loads["q"] = copies.start(r.q_far, r.q)
    for head in range(1, count):
        loads[head] = copies.start(r.e_far.at[head], r.e.at[head])
    here = pl.ds(pl.multiple_of(core * seq, TILE), seq)
    going = [
        copies.start(r.e_far.at[count : 2 * count], r.er),
        copies.start(r.u_far.at[here], r.u),
    ]
    for name in ("v", 0, "k", "q"):
        loads.pop(name).wait()
    for head in range(count):
        cols = head_cols(head)
        if head in loads:
            loads.pop(head).wait()
        head_back(r, head, r.e.at[head], r.dq.at[:, cols], r.dk.at[:, cols], r.dv.at[:, cols])
    for copy in going:
        copy.wait()


def early_heads(core, kept, dm, ir, tokens, after=()):
    seq, width = kept["q"].shape
    keys = kept["k"].shape[0]
    count = width // HEAD_DIM // 2
    arrays = {"q": (seq, width), "k": (keys, width), "v": (keys, width)}
    results = named(
        early_heads_kernel,
        {"core": scalars(core), "u_far": held(tokens)}
        | {name + "_far": held(kept[name]) for name in (*arrays, "e")}
        | {"dm": near(dm), "ir": near(ir)},
        {
            "dq": passed((seq, width // 2)),
            "dk": passed((keys, width // 2)),
            "dv": passed((keys, width // 2)),
            "er": passed((count, keys, seq)),
            "u": passed((seq, width)),
        }
        | {name: passed(dims) for name, dims in arrays.items()},
        {"e": pltpu.VMEM((count, keys, seq), BF), "sm": DMA((16,))},
        "early",
        limit=20,
        flops=110_000_000_000,
        moved=16_000_000,
        after=after,
    )
    return results | {"dm": dm, "ir": ir}


def late_heads_kernel(layer, r):
    core = r.core[0]
    seq, width = r.u.shape
    keys = r.k.shape[0]
    half = width // 2
    heads = width // HEAD_DIM
    copies = Copies(r.sm)
    going = copies.choose(core == layer, both(r, "qkv"), r.wq)
    r.dqkv[:, 0:half] = r.dq[...]
    r.dqkv[0:keys, width : width + half] = r.dk[...]
    r.dqkv[0:keys, 2 * width : 2 * width + half] = r.dv[...]
    for head in range(heads // 2, heads):
        cols = [
            slice(part * width + head * HEAD_DIM, part * width + (head + 1) * HEAD_DIM)
            for part in range(3)
        ]
        head_back(
            r, head, r.er.at[head - heads // 2],
            r.dqkv.at[:, cols[0]], r.dqkv.at[0:keys, cols[1]], r.dqkv.at[0:keys, cols[2]],
        )
    for out_ref, begin in ((r.sd, (1 - core) * half), (r.kp, core * half)):
        rows = pl.ds(pl.multiple_of(begin, half), half)
        out_ref[:, 0:width] = dot_lt(r.u[:, rows], r.dqkv[:, 0:width]).astype(BF)
        out_ref[:, width:] = dot_lt(r.u[0:keys, rows], r.dqkv[0:keys, width:]).astype(BF)
    going.wait()


def late_heads(layer, core, early, weights, after=()):
    seq, width = early["q"].shape
    grads = (width // 2, 3 * width)
    return named(
        functools.partial(late_heads_kernel, layer),
        {"core": scalars(core)}
        | {
            name: near(early[name])
            for name in ("q", "k", "v", "u", "er", "dq", "dk", "dv", "dm", "ir")
        }
        | pairs(weights, "qkv"),
        {
            "sd": passed(grads),
            "kp": passed(grads),
            "dqkv": passed((seq, 3 * width)),
            "wq": passed(weights["qkv"][0].shape),
        },
        {"sm": DMA((1,))},
        "late",
        limit=14,
        flops=110_000_000_000,
        moved=16_000_000,
        after=after,
    )


def heads_kernel(layer, r):
    core = r.core[0]
    seq, width = r.u.shape
    keys = r.k.shape[0]
    copies = Copies(r.sm)
    going = copies.choose(core == layer, both(r, "qkv"), r.wq)
    for head in range(width // HEAD_DIM):
        cols = [
            slice(part * width + head * HEAD_DIM, part * width + (head + 1) * HEAD_DIM)
            for part in range(3)
        ]
        head_back(
            r, head, r.e.at[head],
            r.dqkv.at[:, cols[0]], r.dqkv.at[0:keys, cols[1]], r.dqkv.at[0:keys, cols[2]],
        )
    half = width // 2
    for out_ref, begin in ((r.sd, (1 - core) * half), (r.kp, core * half)):
        rows = pl.ds(pl.multiple_of(begin, half), half)
        out_ref[:, 0:width] = dot_lt(r.u[:, rows], r.dqkv[:, 0:width]).astype(BF)
        out_ref[:, width:] = dot_lt(r.u[0:keys, rows], r.dqkv[0:keys, width:]).astype(BF)
    going.wait()


def all_heads(layer, core, kept, dm, ir, weights, after=()):
    seq, width = kept["q"].shape
    grads = (width // 2, 3 * width)
    return named(
        functools.partial(heads_kernel, layer),
        {"core": scalars(core)}
        | {name: near(kept[name]) for name in ("q", "k", "v", "u", "e")}
        | {"dm": near(dm), "ir": near(ir)}
        | pairs(weights, "qkv"),
        {
            "sd": passed(grads),
            "kp": passed(grads),
            "dqkv": passed((seq, 3 * width)),
            "wq": passed(weights["qkv"][0].shape),
        },
        {"sm": DMA((1,))},
        "heads",
        limit=14,
        flops=220_000_000_000,
        moved=16_000_000,
        after=after,
    )


def input_gradient(dqkv, da, w, keys):
    seq, width = da.shape
    yield slice(0, keys), da[0:keys].astype(F32) + dot_rt(dqkv[0:keys], w[...])
    yield (
        slice(keys, seq),
        da[keys:seq].astype(F32) + dot_rt(dqkv[keys:seq, :width], w[:, :width]),
    )


BACK = ("x2", "s2", "sl", "x1", "s1", "mixed", "inv")


def turn_kernel(coming, r):
    own = r.core[0] == 0
    copies = Copies(r.sm)
    loads = {}
    for name in BACK:
        if name == "sl":
            loads["down"] = copies.choose(own, both(r, "down"), r.w_down)
        loads[name] = copies.start(getattr(r, name + "_in"), getattr(r, name))
        if name == "sl":
            loads["up"] = copies.choose(own, both(r, "up"), r.w_up)
    loads["out"] = copies.choose(own, both(r, "out"), r.w_out)
    going = bring(r, copies, coming)
    vec = jnp.where(own, r.va[...], r.vb[...])
    for rows, values in input_gradient(r.dqkv, r.da_in, r.wq, r.dqkv.shape[0] * 3 // 4):
        r.dy[rows] = values.astype(BF)

    def ready(*names):
        for name in names:
            loads.pop(name).wait()

    ready("x2", "s2")
    feed_back(
        vec, r.dy[...].astype(F32), r.x2, r.s2, r.sl, r.x1, r.s1, r.mixed, r.inv,
        r.w_down, r.w_up, r.w_out, [lambda: ready("down", "sl", "up"), lambda: ready(*list(loads))],
        r.df, r.dz, r.da, r.dm, r.ir, r.small,
    )
    for copy in going:
        copy.wait()


def turn(core, vecs, back, da, kept, weights, coming, after=()):
    seq, width = da.shape
    hidden = weights["up"][0].shape[1]
    wide, narrow = (seq, hidden), (seq, width)
    return named(
        functools.partial(turn_kernel, tuple(coming)),
        {
            "core": scalars(core),
            "va": (vecs[0], IN_VMEM),
            "vb": (vecs[1], IN_VMEM),
            "dqkv": near(back["dqkv"]),
            "da_in": near(da),
            "wq": near(back["wq"]),
        }
        | {name + "_in": held(kept[name]) for name in BACK}
        | pairs(weights, "down", "up", "out")
        | far(coming),
        {
            "df": passed(narrow),
            "dz": passed(wide),
            "da": passed(narrow),
            "dm": passed((width, seq)),
            "ir": passed((8, seq), F32),
            "small": passed((width, LANES)),
        }
        | brought(coming),
        {name: pltpu.VMEM(kept[name].shape, kept[name].dtype) for name in BACK}
        | {f"w_{name}": pltpu.VMEM(weights[name][0].shape, BF) for name in ("down", "up", "out")}
        | {"dy": pltpu.VMEM(narrow, BF), "sm": DMA((24,))},
        "turn",
        limit=36,
        flops=180_000_000_000,
        moved=16_000_000,
        after=after,
    )


def grads_kernel(r):
    feed_grads(
        r.core[0], r.g, r.df, r.h, r.dz, r.mixed, r.da, r.small, r.sd, r.kp
    )


def first_grads(core, back, after=()):
    seq, width = back["df"].shape
    hidden = back["dz"].shape[1]
    grads = (width // 2, 2 * hidden + width + LANES)
    return named(
        grads_kernel,
        {"core": scalars(core)}
        | {name: near(back[name + "_near"]) for name in ("h", "mixed", "g")}
        | {name: near(back[name]) for name in ("df", "dz", "da", "small")},
        {"sd": passed(grads), "kp": passed(grads)},
        {},
        "grads",
        limit=14,
        flops=120_000_000_000,
        moved=10_000_000,
        after=after,
    )


def last_kernel(r):
    seq, width = r.da.shape
    keys = seq * 3 // 4
    half = width // 2
    core = r.core[0]
    for out_ref, begin in ((r.sd, (1 - core) * half), (r.kp, core * half)):
        cols = pl.ds(pl.multiple_of(begin, half), half)
        out_ref[0:keys] = (
            r.da[0:keys, cols].astype(F32) + dot_rt(r.dqkv[0:keys], r.wq[cols])
        ).astype(BF)
        out_ref[keys:seq] = (
            r.da[keys:seq, cols].astype(F32)
            + dot_rt(r.dqkv[keys:seq, :width], r.wq[cols, :width])
        ).astype(BF)


def input_back(core, back, da, after=()):
    return named(
        last_kernel,
        {
            "core": scalars(core),
            "dqkv": near(back["dqkv"]),
            "da": near(da),
            "wq": near(back["wq"]),
        },
        {name: passed((da.shape[0], da.shape[1] // 2)) for name in ("sd", "kp")},
        {},
        "input",
        limit=8,
        flops=50_000_000_000,
        moved=6_000_000,
        after=after,
    )


def stages(count):
    bits = count.bit_length() - 1
    first = (bits - 1) // 3
    one = list(range(bits))
    two = one[first : 2 * first] + one[:first] + one[2 * first :]
    return list(zip(one, two))


def exchange(block, bits):
    count = lax.axis_size(DP)
    route = [
        (place * 2 + core, (place ^ 1 << bits[core]) * 2 + core)
        for place in range(count)
        for core in (0, 1)
    ]
    return lax.ppermute(block, (DP, SECTION), route)


def across(block):
    return lax.ppermute(block, SECTION, [(0, 1), (1, 0)])


def combine_kernel(stage, bits_ref, keep_ref, come_ref, *outs):
    if stage is None:
        outs[0][...] = (keep_ref[...].astype(F32) + come_ref[...].astype(F32)).astype(BF)
        return
    half = keep_ref.shape[0] // 2
    mine = bits_ref[stage] * half
    for out_ref, start in zip(outs, (half - mine, mine)):
        place = pl.ds(pl.multiple_of(start, TILE), half)
        out_ref[...] = (keep_ref[place].astype(F32) + come_ref[place].astype(F32)).astype(BF)


def combine(bits, stage, kp, come, after=()):
    rows, width = kp.shape
    outs = [shape((rows, width))] if stage is None else [shape((rows // 2, width))] * 2
    return call(
        functools.partial(combine_kernel, stage),
        "combine",
        [scalars(bits), (kp, IN_VMEM), (come, IN_VMEM)],
        [(out, IN_VMEM) for out in outs],
        limit=8,
        flops=STEP,
        after=after,
    )


def finish_kernel(*refs):
    out_ref = refs[-1]
    at = 0
    for keep_ref, come_ref in zip(refs[:-1:2], refs[1:-1:2]):
        width = keep_ref.shape[1]
        out_ref[:, at : at + width] = (
            keep_ref[...].astype(F32) + come_ref[...].astype(F32)
        ).astype(BF)
        at += width


def merge_kernel(stage, bits_ref, own_ref, come_ref, out_ref):
    rows = own_ref.shape[0]
    mine = bits_ref[stage] * rows
    out_ref[pl.ds(pl.multiple_of(mine, TILE), rows)] = own_ref[...]
    out_ref[pl.ds(pl.multiple_of(rows - mine, TILE), rows)] = come_ref[...]


def merge(bits, stage, own, come, after=()):
    rows, width = own.shape
    return call(
        functools.partial(merge_kernel, stage),
        "merge",
        [scalars(bits), (own, IN_VMEM), (come, IN_VMEM)],
        [(shape((2 * rows, width)), IN_VMEM)],
        limit=8,
        flops=STEP,
        after=after,
    )[0]


class Sums:
    def __init__(self, bits, arrays, halvings, turned):
        self.bits = bits
        self.turned = turned
        self.plan = stages(lax.axis_size(DP))
        if turned:
            first = (len(self.plan) - 1) // 3
            self.plan = (
                self.plan[first : 2 * first] + self.plan[:first] + self.plan[2 * first :]
            )
        self.halvings = halvings
        self.block = arrays["kp"]
        self.come = across(arrays["sd"])
        self.stage = 0
        self.halved = []
        self.doubling = False

    def place(self, stage):
        count = len(self.plan)
        first = (count - 1) // 3
        if self.turned and stage < 2 * first:
            stage = (stage + first) % (2 * first)
        return BITS + stage

    def left(self):
        return self.come is not None

    def step(self, after=()):
        if self.doubling:
            self.block = merge(self.bits, self.place(self.halved.pop()), self.block, self.come, after)
            return self.double()
        if self.stage == len(self.plan):
            (self.block,) = combine(self.bits, None, self.block, self.come, after)
            self.doubling = True
            return self.double()
        if self.stage >= self.halvings or self.block.shape[0] % (2 * TILE):
            (self.block,) = combine(self.bits, None, self.block, self.come, after)
            sd = self.block
        else:
            place = self.place(self.stage)
            sd, self.block = combine(self.bits, place, self.block, self.come, after)
            self.halved.append(self.stage)
        self.come = exchange(sd, self.plan[self.stage])
        self.stage += 1
        return (sd,)

    def double(self):
        self.come = exchange(self.block, self.plan[self.halved[-1]]) if self.halved else None
        return (self.block,)


def place_kernel(core_ref, keep_ref, come_ref, out_ref, mark_ref):
    rows = keep_ref.shape[0]
    mark_ref[...] = jnp.zeros_like(mark_ref)

    @pl.when(core_ref[0] == 0)
    def _():
        out_ref[0:rows] = keep_ref[...]
        out_ref[rows:] = come_ref[...]

    @pl.when(core_ref[0] == 1)
    def _():
        out_ref[0:rows] = come_ref[...]
        out_ref[rows:] = keep_ref[...]


def place_halves(core, kp, come, after=()):
    rows, width = kp.shape
    return call(
        place_kernel,
        "place",
        [scalars(core), (kp, IN_VMEM), (come, IN_VMEM)],
        [(shape((2 * rows, width)), IN_VMEM), (shape((8, LANES), F32), IN_VMEM)],
        limit=8,
        flops=STEP,
        after=after,
    )


def collect_kernel(count, mine, parts, r):
    half = r.one.shape[0]
    r.mark[...] = jnp.zeros_like(r.mark)

    def write(ref, begin):
        copies = Copies(r.sm)
        going = []
        at = 0
        for name, offset, width in parts:
            cols = slice(at, at + width)
            r.hold[:, cols] = ref[:, cols].astype(F32)
            target = getattr(r, name).at[0, offset + begin : offset + begin + half]
            going.append(copies.start(r.hold.at[:, cols], target))
            at += width
        for copy in going:
            copy.wait()

    def vectors(own_ref, come_ref, begin):
        at = sum(width for _, _, width in parts)
        for ref, place in ((own_ref, begin), (come_ref, half - begin)):
            small = ref[:, at:].astype(F32).T
            for row in range(count):
                width = r.out.shape[2]
                r.b_up[:, row * width + place : row * width + place + half] = small[row : row + 1]
            for row, name in enumerate(("bd", "g1", "c1", "g2", "c2")):
                getattr(r, name)[:, place : place + half] = small[count + row : count + row + 1]

    @pl.when(r.core[0] == 0)
    def _():
        if count:
            vectors(r.one_own, r.one, 0)
        write(r.one, 0 if mine else half)

    @pl.when(r.core[0] == 1)
    def _():
        if count:
            vectors(r.two_own, r.two, half)
        write(r.two, half if mine else 0)


def collect(core, one, two, outs, parts, name, after=(), begun=None, own=None, small=None):
    half = one.shape[0]
    begun = begun or {}
    ins = {"core": scalars(core), "one": (one, IN_VMEM), "two": (two, IN_VMEM)}
    if small:
        ins |= {"one_own": (own[0], IN_VMEM), "two_own": (own[1], IN_VMEM)}
    ins |= {name + "_begun": (array, ANYWHERE) for name, array in begun.items()}
    results = {name: (shape(dims, F32), ANYWHERE) for name, dims in outs.items()}
    results |= {name: (shape(dims, F32), IN_VMEM) for name, dims in (small or {}).items()}
    results["mark"] = (shape((8, LANES), F32), IN_VMEM)
    scratch = {
        "hold": pltpu.VMEM((half, sum(width for _, _, width in parts)), F32),
        "sm": DMA((len(parts),)),
    }
    names = list(ins) + list(results) + list(scratch)
    count = len(ins)
    first = count - len(begun)
    rows = small["b_up"][1] // small["bd"][1] if small else 0

    def run(*refs):
        collect_kernel(rows, not begun, parts, Refs(names, refs[:count] + refs[count + len(after) :]))

    values = pl.pallas_call(
        run,
        out_shape=[out for out, _ in results.values()],
        in_specs=[spec for _, spec in ins.values()] + [ANYWHERE] * len(after),
        out_specs=[spec for _, spec in results.values()],
        scratch_shapes=list(scratch.values()),
        input_output_aliases={first + place: place for place in range(len(begun))},
        compiler_params=pltpu.CompilerParams(vmem_limit_bytes=16 * MIB),
        cost_estimate=pl.CostEstimate(flops=STEP, bytes_accessed=0, transcendentals=0),
        name=name,
    )(*[array for array, _ in ins.values()], *after)
    return dict(zip(results, values))


def pack_kernel(r):
    copies = Copies(r.sm)
    names = ("b_up", "bd", "g1", "c1", "g2", "c2")
    going = [copies.start(getattr(r, name), getattr(r, name + "_hold")) for name in names]
    for copy in going:
        copy.wait()
    width = r.bd.shape[1]
    parts = r.b_up.shape[1] // width
    r.out[...] = jnp.zeros_like(r.out)
    for part in range(parts):
        r.out[part : part + 1] = r.b_up_hold[:, part * width : (part + 1) * width]
    for place, name in enumerate(names[1:]):
        r.out[parts + place : parts + place + 1] = getattr(r, name + "_hold")[...]


def pack(b_up, bd, g1, c1, g2, c2):
    arrays = {"b_up": b_up, "bd": bd, "g1": g1, "c1": c1, "g2": g2, "c2": c2}
    return named(
        pack_kernel,
        {name: held(array) for name, array in arrays.items()},
        {"out": (shape((8, bd.shape[1]), F32), IN_VMEM)},
        {name + "_hold": pltpu.VMEM(array.shape, F32) for name, array in arrays.items()}
        | {"sm": DMA((6,))},
        "pack",
        limit=4,
        flops=0,
        moved=20_000,
    )["out"]


def body(
    tokens, cotangent, lengths, train_counts,
    wq, w_out, w_up, b_up, w_down, bd, gain_one, bias_one, gain_two, bias_two,
):
    index = lax.axis_index(SECTION)
    place = lax.axis_index(DP)
    at_first = index == 0
    seq = tokens.shape[0] // lengths.shape[0]
    width = tokens.shape[1]
    hidden = w_up.shape[2]
    plan = stages(lax.axis_size(DP))
    first_bit = jnp.array([one for one, _ in plan], jnp.int32)
    other_bit = jnp.array([two for _, two in plan], jnp.int32)
    core = bits = jnp.concatenate(
        [
            index[None].astype(jnp.int32),
            place >> jnp.where(at_first, first_bit, other_bit) & 1,
        ]
    )
    weights = {"qkv": (wq[0], across(wq[0]))}
    vec = pack(b_up, bd, gain_one, bias_one, gain_two, bias_two)
    later = lax.optimization_barrier((w_out[0], w_up[0], w_down[0], vec))[:3]
    weights |= {name: (array, across(array)) for name, array in zip(("out", "up", "down"), later)}
    vecs = (vec, across(vec))

    first = attend_first(core, seq, train_counts, tokens, weights)
    kept = middle(core, train_counts, lengths, cotangent, vecs, first, weights)
    kept["u"] = kept["y"]
    kept_one = {name: kept[name] for name in KEPT} | {
        "mixed": kept["mo"], "inv": kept["io"],
        "q": first["q"], "k": first["k"], "v": first["v"], "e": first["e"],
    }

    def some(*names):
        return {name: kept_one[name] for name in names}

    sums = {A2: Sums(bits, kept, *PLANS[A2])}
    last_come = across(kept["ls"])
    vectors = {"b_up": (1, hidden)} | {
        name: (1, width) for name in ("bd", "g1", "c1", "g2", "c2")
    }
    feed_outs = {"up": (1, width, hidden), "out": (1, width, width), "down": (1, hidden, width)}
    feed_parts = [("up", 0, hidden), ("out", 0, width)]
    feed_parts += [("down", place * width, width) for place in range(hidden // width)]

    def come(one, two):
        return lax.ppermute(one, SECTION, [(1, 0)]), lax.ppermute(two, SECTION, [(0, 1)])

    mark = (kept["sd"],)
    for name in ORDER:
        if name == HEADS:
            two = all_heads(1, core, kept, kept["dm"], kept["ir"], weights, mark)
            sums[B2] = Sums(bits, two, *PLANS[B2])
            mark = (two["sd"],)
        elif name == TURN:
            back = turn(
                core, vecs, two, kept["da"], kept_one, weights, some("h", "g", "mixed"), mark
            )
            mark = (back["df"],)
        elif name == GRADS:
            grads = first_grads(core, back, mark)
            sums[A1] = Sums(bits, grads, *PLANS[A1])
            mark = (grads["sd"],)
        elif name == EARLY:
            early = early_heads(core, kept_one, back["dm"], back["ir"], tokens, mark)
            mark = (early["dq"],)
        elif name == LATE:
            one = late_heads(0, core, early, weights, mark)
            sums[B1] = Sums(bits, one, *PLANS[B1])
            mark = (one["sd"],)
        elif name == INPUT:
            du = input_back(core, one, back["da"], mark)
            du_come = across(du["sd"])
            mark = (du["sd"],)
        elif name == OUT:
            output, *mark = place_halves(core, kept["lk"], last_come, mark)
        elif name == IN:
            grad_tokens, *mark = place_halves(core, du["kp"], du_come, mark)
        elif name == OWN:
            while sums[A1].left():
                mark = sums[A1].step(mark)
            while sums[A2].left():
                mark = sums[A2].step(mark)
            fed = sums[A1].block, sums[A2].block
            fed_come = come(*fed)
            feed_begun = collect(core, *fed, feed_outs, feed_parts, "own", mark)
            mark = (feed_begun.pop("mark"),)
        elif name == COME:
            feed_done = collect(
                core, *fed_come, feed_outs, feed_parts, "come", mark, feed_begun, fed, vectors
            )
            mark = (feed_done.pop("mark"),)
        elif sums[name].left():
            mark = sums[name].step(mark)
    qkv_outs, qkv_parts = {"qkv": (1, width, 3 * width)}, [("qkv", 0, 3 * width)]
    for name in (B2, B1):
        while sums[name].left():
            mark = sums[name].step(mark)
    qkv = sums[B1].block, sums[B2].block
    qkv_come = come(*qkv)
    qkv_begun = collect(core, *qkv, qkv_outs, qkv_parts, "own", mark)
    del qkv_begun["mark"]
    grad_w_qkv = collect(core, *qkv_come, qkv_outs, qkv_parts, "come", (), qkv_begun)["qkv"]
    grad_w_up, grad_w_out, grad_w_down, *grad_vectors = feed_done.values()
    grad_b_up, grad_b_down, *grad_norms = grad_vectors
    return (
        output,
        grad_tokens,
        grad_w_qkv,
        grad_w_out,
        grad_w_up,
        grad_b_up,
        grad_w_down,
        grad_b_down,
        *grad_norms,
    )


def solution(mesh):
    matrix = P(SECTION, None, None)
    vector = P(SECTION, None)
    weights = (matrix, matrix, matrix, vector, matrix, vector, vector, vector, vector, vector)
    rows = P(DP, None)
    halves = P(DP, SECTION)
    return jax.shard_map(
        body,
        mesh=mesh,
        in_specs=(rows, rows, P(DP), P(DP)) + weights,
        out_specs=(halves, halves) + weights,
        check_vma=False,
    )
```

```python
import functools

import jax
import jax.numpy as jnp
from jax import lax
from jax.experimental import pallas as pl
from jax.experimental.pallas import tpu as pltpu
from jax.sharding import PartitionSpec as P

HEAD_DIM = 128
EPS = 1e-05
LOG2E = 1.4426950408889634
ROOT = 0.7978845608028654
CUBE = 0.044715
BF = jnp.bfloat16
DP, SECTION = "dp", "section"
F32 = jnp.float32
TILE = 16
STEP = 8_000_000_000
CORE, BITS = 0, 1
LANES = 128
MIB = 1 << 20

IN_VMEM = pl.BlockSpec(memory_space=pltpu.VMEM)
IN_SMEM = pl.BlockSpec(memory_space=pltpu.SMEM)
ANYWHERE = pl.BlockSpec(memory_space=pl.ANY)
IN_HBM = pl.BlockSpec(memory_space=pltpu.HBM)
DMA = pltpu.SemaphoreType.DMA


def shape(dims, kind=BF):
    return jax.ShapeDtypeStruct(dims, kind)


def call(kernel, name, operands, outs, scratch=(), limit=24, flops=0, moved=0, after=()):
    count = len(operands)

    def run(*refs):
        kernel(*refs[:count], *refs[count + len(after) :])

    return pl.pallas_call(
        run,
        out_shape=[out for out, _ in outs],
        in_specs=[spec for _, spec in operands] + [ANYWHERE] * len(after),
        out_specs=[spec for _, spec in outs],
        scratch_shapes=list(scratch),
        compiler_params=pltpu.CompilerParams(vmem_limit_bytes=limit * MIB),
        cost_estimate=pl.CostEstimate(flops=flops, bytes_accessed=moved, transcendentals=0),
        name=name,
    )(*[array for array, _ in operands], *after)


def product(left, right, over):
    return lax.dot_general(left, right, (over, ((), ())), preferred_element_type=F32)


def dot(left, right):
    return product(left, right, ((1,), (0,)))


def dot_rt(left, right):
    return product(left, right, ((1,), (1,)))


def dot_lt(left, right):
    return product(left, right, ((0,), (0,)))


def mean(block):
    return jnp.mean(block, axis=1, keepdims=True)


def down(block):
    return jnp.sum(block, axis=0, keepdims=True)


def normed(block):
    centred = block - mean(block)
    scale = lax.rsqrt(mean(centred * centred) + EPS)
    return centred * scale, scale


class Copies:
    def __init__(self, sm):
        self.sm = sm
        self.used = 0

    def start(self, source, target):
        copy = pltpu.make_async_copy(source, target, self.sm.at[self.used])
        self.used += 1
        copy.start()
        return copy

    def choose(self, own, refs, target, cols=None):
        sem = self.sm.at[self.used]
        self.used += 1
        if cols is not None:
            refs = [ref.at[:, cols] for ref in refs]
            target = target.at[:, cols]

        @pl.when(own)
        def _():
            pltpu.make_async_copy(refs[0], target, sem).start()

        @pl.when(jnp.logical_not(own))
        def _():
            pltpu.make_async_copy(refs[1], target, sem).start()

        return pltpu.make_async_copy(refs[0], target, sem)


class Refs:
    def __init__(self, names, refs):
        self.__dict__.update(zip(names, refs, strict=True))


def named(kernel, ins, outs, scratch, name, limit, flops, moved, after=()):
    names = list(ins) + list(outs) + list(scratch)

    def run(*refs):
        kernel(Refs(names, refs))

    results = call(
        run,
        name,
        list(ins.values()),
        list(outs.values()),
        list(scratch.values()),
        limit=limit,
        flops=flops,
        moved=moved,
        after=after,
    )
    return dict(zip(outs, results))


def pairs(weights, *names):
    return {
        f"{name}_{which}": held(array) if which == "own" else (array, ANYWHERE)
        for name in names
        for which, array in zip(("own", "other"), weights[name])
    }


def both(r, name):
    return [getattr(r, name + "_own"), getattr(r, name + "_other")]


def stored(dims, kind=BF):
    return (pltpu.HBM(dims, kind), IN_HBM)


def passed(dims, kind=BF):
    return (shape(dims, kind), IN_VMEM)


def held(array):
    return (pltpu.with_memory_space_constraint(array, pltpu.HBM), IN_HBM)


def near(array):
    return (array, IN_VMEM)


def scalars(array):
    return (array, IN_SMEM)


def head_cols(head):
    return slice(head * HEAD_DIM, (head + 1) * HEAD_DIM)


def attention(copies, count, u, w, waits, q, k, v, inv, mixed, e, e_out, early=lambda: []):
    seq, width = u.shape
    keys = k.shape[0]
    factor = HEAD_DIM**-0.5 * LOG2E
    waits[0]()
    k[...] = dot(u[0:keys], w[:, width : 2 * width]).astype(BF)
    waits[1]()
    v[...] = dot(u[0:keys], w[:, 2 * width :]).astype(BF)
    waits[2]()
    q[...] = dot(u[...], w[:, :width]).astype(BF)
    saves = early()
    places = lax.broadcasted_iota(jnp.int32, (keys, 1), 0)
    bias = jnp.where(places < count(), 0.0, -1e30).astype(F32)
    for head in range(width // HEAD_DIM):
        cols = head_cols(head)
        scores = dot_rt(k[:, cols], q[:, cols]) * factor + bias
        powers = jnp.exp2(scores - jnp.max(scores, axis=0, keepdims=True))
        scale = 1.0 / down(powers)
        inv[head : head + 1] = scale
        low = powers.astype(BF)
        e[head] = low
        if e_out is not None:
            saves.append(copies.start(e.at[head], e_out.at[head]))
        mixed[cols] = (dot(v[:, cols].T, low) * scale).astype(BF)
    return saves


def feed(vec, u, mixed, w_out, w_up, w_down, ready, x1_ref, s1_ref, h_ref, g_ref, slope_ref, x2_ref, s2_ref):
    width, hidden = w_up.shape
    ready[0]()
    a = u[...].astype(F32) + dot_lt(mixed[...], w_out[...])
    x1, s1 = normed(a)
    x1_ref[...] = x1.astype(BF)
    s1_ref[...] = s1
    h = x1 * vec[3:4] + vec[4:5]
    h_low = h.astype(BF)
    h_ref[...] = h_low
    f = h + vec[2:3]
    ready[1]()
    ready[2]()
    for part in range(hidden // width):
        cols = slice(part * width, (part + 1) * width)
        z = (dot(h_low, w_up[:, cols]) + vec[part : part + 1]).astype(BF)
        square = z * z
        curve = jnp.tanh(z * (ROOT + ROOT * CUBE * square))
        gate = 0.5 * curve + 0.5
        g = z * gate
        g_ref[:, cols] = g
        steep = (0.5 * z) * (1.0 - curve * curve) * (ROOT + 3 * ROOT * CUBE * square)
        slope_ref[:, cols] = gate + steep
        f = f + dot(g, w_down[cols])
    x2, s2 = normed(f)
    x2_ref[...] = x2.astype(BF)
    s2_ref[...] = s2
    return x2 * vec[5:6] + vec[6:7]


def feed_back(vec, dy, x2, s2, sl, x1, s1, mixed, inv, w_down, w_up, w_out, ready, df_ref, dz_ref, da_ref, dm_ref, inner_ref, small_ref):
    seq, width = dy.shape
    hidden = w_up.shape[1]
    x2 = x2[...].astype(F32)
    small = [None] * 7
    small[6] = down(dy)
    small[5] = down(dy * x2)
    t = dy * vec[5:6]
    df = s2[...] * (t - mean(t) - x2 * mean(t * x2))
    small[2] = down(df)
    df_low = df.astype(BF)
    df_ref[...] = df_low
    dh = df
    ready[0]()
    for part in range(hidden // width):
        cols = slice(part * width, (part + 1) * width)
        dz = (dot_rt(df_low, w_down[cols]) * sl[:, cols].astype(F32)).astype(BF)
        dz_ref[:, cols] = dz
        small[part] = down(dz.astype(F32))
        dh = dh + dot_rt(dz, w_up[:, cols])
    ready[1]()
    x1 = x1[...].astype(F32)
    small[4] = down(dh)
    small[3] = down(dh * x1)
    t = dh * vec[3:4]
    da = (s1[...] * (t - mean(t) - x1 * mean(t * x1))).astype(BF)
    da_ref[...] = da
    inner_ref[...] = jnp.zeros_like(inner_ref)
    for head in range(width // HEAD_DIM):
        cols = head_cols(head)
        low = (dot_rt(w_out[cols], da) * inv[head : head + 1]).astype(BF)
        inner_ref[head : head + 1] = down(low.astype(F32) * mixed[cols].astype(F32))
        dm_ref[cols] = low
    bottom = jnp.concatenate(small + [jnp.zeros((LANES - 7, width), F32)], axis=0)
    small_ref[...] = bottom.T.astype(BF)


def feed_grads(core, g, df, h, dz, mixed, da, small, send_ref, keep_ref):
    seq, width = df.shape
    hidden = g.shape[1]
    half = width // 2
    for out_ref, begin in ((send_ref, (1 - core) * half), (keep_ref, core * half)):
        begin = pl.multiple_of(begin, half)
        rows = pl.ds(begin, half)
        out_ref[:, 0:hidden] = dot_lt(h[:, rows], dz[...]).astype(BF)
        at = hidden
        out_ref[:, at : at + width] = dot(mixed[rows], da[...]).astype(BF)
        for part in range(hidden // width):
            at += width
            these = pl.ds(pl.multiple_of(begin + part * width, half), half)
            out_ref[:, at : at + width] = dot_lt(g[:, these], df[...]).astype(BF)
        out_ref[:, at + width :] = small[rows]


def first_kernel(r):
    core = r.core[0]
    seq, width = r.u.shape
    copies = Copies(r.sm)
    rows = copies.start(r.tokens.at[pl.ds(pl.multiple_of(core * seq, TILE), seq)], r.u)
    parts = [
        copies.choose(core == 0, both(r, "qkv"), r.w, slice(part * width, (part + 1) * width))
        for part in (1, 2, 0)
    ]

    def begin():
        rows.wait()
        parts[0].wait()

    counting = copies.start(r.counts, r.cn)

    def count():
        counting.wait()
        return r.cn[core]

    saves = attention(
        copies, count, r.u, r.w, [begin, parts[1].wait, parts[2].wait],
        r.q_hold, r.k_hold, r.v_hold, r.inv, r.mixed, r.e_hold, r.e,
        lambda: [
            copies.start(getattr(r, name + "_hold"), getattr(r, name)) for name in ("q", "k", "v")
        ],
    )
    for save in saves:
        save.wait()


def attend_first(core, seq, counts, tokens, weights):
    width = tokens.shape[1]
    keys = seq * 3 // 4
    heads = width // HEAD_DIM
    return named(
        first_kernel,
        {"core": scalars(core), "counts": held(counts), "tokens": held(tokens)}
        | pairs(weights, "qkv"),
        {
            "q": stored((seq, width)),
            "k": stored((keys, width)),
            "v": stored((keys, width)),
            "e": stored((heads, keys, seq)),
            "inv": passed((8, seq), F32),
            "mixed": passed((width, seq)),
            "u": passed((seq, width)),
        },
        {
            "w": pltpu.VMEM((width, 3 * width), BF),
            "q_hold": pltpu.VMEM((seq, width), BF),
            "k_hold": pltpu.VMEM((keys, width), BF),
            "v_hold": pltpu.VMEM((keys, width), BF),
            "e_hold": pltpu.VMEM((heads, keys, seq), BF),
            "cn": pltpu.SMEM(counts.shape, jnp.int32),
            "sm": DMA((16,)),
        },
        "first",
        limit=26,
        flops=160_000_000_000,
        moved=10_000_000,
    )


A2, B2, A1, B1, HEADS, TURN, GRADS, EARLY, LATE, INPUT, OUT, IN, OWN, COME = range(14)
PLANS = {A2: (3, False), B2: (3, False), A1: (3, True), B1: (2, True)}
ORDER = (
    HEADS, A2, TURN, A2, B2, GRADS, A2, EARLY, A1, B2, A2, LATE, A1, B2,
    A2, INPUT, B1, A1, A2, B2, A1, B1, OUT, IN, B1, B2, A2, A1,
    B1, B2, A1, A2, B2, B1, A1, B2, B1, A1, OWN, COME, B1,
)
KEPT = ("x1", "s1", "h", "g", "sl", "x2", "s2")


def middle_kernel(r):
    core = r.core[0]
    seq, width = r.u.shape
    copies = Copies(r.sm)
    own = core == 0
    here = pl.ds(pl.multiple_of(core * seq, TILE), seq)
    ready = [
        copies.choose(own, both(r, "out"), r.w_out),
        copies.choose(own, both(r, "up"), r.w_up),
        copies.choose(own, both(r, "down"), r.w_down),
    ]
    qkv = [
        copies.choose(
            jnp.logical_not(own), both(r, "qkv"), r.wq, slice(part * width, (part + 1) * width)
        )
        for part in (1, 2, 0)
    ]
    ready_two = [
        copies.choose(jnp.logical_not(own), both(r, "out"), r.w_out_two),
        copies.choose(jnp.logical_not(own), both(r, "up"), r.w_up_two),
        copies.choose(jnp.logical_not(own), both(r, "down"), r.w_down_two),
    ]
    counting = copies.start(r.counts, r.cn)
    measuring = copies.start(r.lengths, r.ln)
    incoming = copies.start(r.ct.at[here], r.dy)
    saves = [copies.start(r.mixed, r.mo), copies.start(r.inv, r.io)]
    one = jnp.where(own, r.va[...], r.vb[...])
    two = jnp.where(own, r.vb[...], r.va[...])
    y = feed(
        one, r.u, r.mixed, r.w_out, r.w_up, r.w_down,
        [copy.wait for copy in ready],
        *[getattr(r, "new_" + name) for name in KEPT],
    )
    r.y[...] = y.astype(BF)
    for name in KEPT:
        saves.append(copies.start(getattr(r, "new_" + name), getattr(r, name)))
    early, saves = saves, []
    counting.wait()
    attention(
        copies, lambda: r.cn[core], r.y, r.wq, [copy.wait for copy in qkv],
        r.q, r.k, r.v, r.inv_two, r.mixed_two, r.e, None,
    )
    for save in early:
        save.wait()
    y = feed(
        two, r.y, r.mixed_two, r.w_out_two, r.w_up_two, r.w_down_two,
        [copy.wait for copy in ready_two],
        *[getattr(r, "new_" + name) for name in KEPT],
    )
    places = lax.broadcasted_iota(jnp.int32, (seq, 1), 0)
    measuring.wait()
    valid = places < r.ln[core]
    r.last[...] = jnp.where(valid, y, 0.0).astype(BF)
    half = width // 2
    for out_ref, begin in ((r.ls, (1 - core) * half), (r.lk, core * half)):
        out_ref[...] = r.last[:, pl.ds(pl.multiple_of(begin, half), half)]
    incoming.wait()
    dy = jnp.where(valid, r.dy[...].astype(F32), 0.0)
    nothing = [lambda: None] * 2
    feed_back(
        two, dy, r.new_x2, r.new_s2, r.new_sl, r.new_x1, r.new_s1, r.mixed_two, r.inv_two,
        r.w_down_two, r.w_up_two, r.w_out_two, nothing, r.df, r.dz, r.da, r.dm, r.ir, r.small,
    )
    feed_grads(
        core, r.new_g, r.df, r.new_h, r.dz, r.mixed_two, r.da, r.small, r.sd, r.kp
    )
    for save in saves:
        save.wait()


def middle(core, counts, lengths, cotangent, vecs, first, weights):
    seq, width = first["u"].shape
    keys = seq * 3 // 4
    heads = width // HEAD_DIM
    hidden = weights["up"][0].shape[1]
    wide, narrow, tall = (seq, hidden), (seq, width), (seq, 1)
    kept = {
        "x1": (narrow, BF), "s1": (tall, F32), "h": (narrow, BF), "g": (wide, BF),
        "sl": (wide, BF), "x2": (narrow, BF), "s2": (tall, F32),
    }
    grads = (width // 2, 2 * hidden + width + LANES)
    return named(
        middle_kernel,
        {
            "core": scalars(core),
            "counts": held(counts),
            "lengths": held(lengths),
            "ct": held(cotangent),
            "va": (vecs[0], IN_VMEM),
            "vb": (vecs[1], IN_VMEM),
            "mixed": near(first["mixed"]),
            "inv": near(first["inv"]),
            "u": near(first["u"]),
        }
        | pairs(weights, "qkv", "out", "up", "down"),
        {name: stored(*what) for name, what in kept.items()}
        | {
            "mo": stored((width, seq)),
            "io": stored((8, seq), F32),
            "ls": passed((seq, width // 2)),
            "lk": passed((seq, width // 2)),
            "y": passed(narrow),
            "q": passed(narrow),
            "k": passed((keys, width)),
            "v": passed((keys, width)),
            "e": passed((heads, keys, seq)),
            "da": passed(narrow),
            "dm": passed((width, seq)),
            "ir": passed((8, seq), F32),
            "sd": passed(grads),
            "kp": passed(grads),
        },
        {f"new_{name}": pltpu.VMEM(*what) for name, what in kept.items()}
        | {
            "dy": pltpu.VMEM(narrow, BF),
            "last": pltpu.VMEM(narrow, BF),
            "cn": pltpu.SMEM(counts.shape, jnp.int32),
            "ln": pltpu.SMEM(lengths.shape, jnp.int32),
            "inv_two": pltpu.VMEM((8, seq), F32),
            "mixed_two": pltpu.VMEM((width, seq), BF),
            "df": pltpu.VMEM(narrow, BF),
            "dz": pltpu.VMEM(wide, BF),
            "small": pltpu.VMEM((width, LANES), BF),
            "wq": pltpu.VMEM((width, 3 * width), BF),
        }
        | {
            f"w_{name}{end}": pltpu.VMEM(weights[name][0].shape, BF)
            for name in ("out", "up", "down")
            for end in ("", "_two")
        }
        | {"sm": DMA((32,))},
        "middle",
        limit=32,
        flops=600_000_000_000,
        moved=60_000_000,
    )


def bring(r, copies, names):
    return [copies.start(getattr(r, name + "_far"), getattr(r, name + "_near")) for name in names]


def far(arrays):
    return {name + "_far": held(array) for name, array in arrays.items()}


def brought(arrays):
    return {name + "_near": passed(array.shape, array.dtype) for name, array in arrays.items()}


def head_back(r, head, powers, out_q, out_k, out_v):
    cols = head_cols(head)
    scale = HEAD_DIM**-0.5
    change = dot(r.v[:, cols], r.dm[cols]) - r.ir[head : head + 1]
    ds = (powers[...].astype(F32) * change).astype(BF)
    out_v[...] = dot(powers[...], r.dm[cols].T).astype(BF)
    out_q[...] = (dot(r.k[:, cols].T, ds) * scale).T.astype(BF)
    out_k[...] = (dot(ds, r.q[:, cols]) * scale).astype(BF)


def early_heads_kernel(r):
    core = r.core[0]
    seq = r.dm.shape[1]
    count = r.dq.shape[1] // HEAD_DIM
    copies = Copies(r.sm)
    loads = {"v": copies.start(r.v_far, r.v), 0: copies.start(r.e_far.at[0], r.e.at[0])}
    loads["k"] = copies.start(r.k_far, r.k)
    loads["q"] = copies.start(r.q_far, r.q)
    for head in range(1, count):
        loads[head] = copies.start(r.e_far.at[head], r.e.at[head])
    here = pl.ds(pl.multiple_of(core * seq, TILE), seq)
    going = [
        copies.start(r.e_far.at[count : 2 * count], r.er),
        copies.start(r.u_far.at[here], r.u),
    ]
    for name in ("v", 0, "k", "q"):
        loads.pop(name).wait()
    for head in range(count):
        cols = head_cols(head)
        if head in loads:
            loads.pop(head).wait()
        head_back(r, head, r.e.at[head], r.dq.at[:, cols], r.dk.at[:, cols], r.dv.at[:, cols])
    for copy in going:
        copy.wait()


def early_heads(core, kept, dm, ir, tokens, after=()):
    seq, width = kept["q"].shape
    keys = kept["k"].shape[0]
    count = width // HEAD_DIM // 2
    arrays = {"q": (seq, width), "k": (keys, width), "v": (keys, width)}
    results = named(
        early_heads_kernel,
        {"core": scalars(core), "u_far": held(tokens)}
        | {name + "_far": held(kept[name]) for name in (*arrays, "e")}
        | {"dm": near(dm), "ir": near(ir)},
        {
            "dq": passed((seq, width // 2)),
            "dk": passed((keys, width // 2)),
            "dv": passed((keys, width // 2)),
            "er": passed((count, keys, seq)),
            "u": passed((seq, width)),
        }
        | {name: passed(dims) for name, dims in arrays.items()},
        {"e": pltpu.VMEM((count, keys, seq), BF), "sm": DMA((16,))},
        "early",
        limit=20,
        flops=110_000_000_000,
        moved=16_000_000,
        after=after,
    )
    return results | {"dm": dm, "ir": ir}


def late_heads_kernel(layer, r):
    core = r.core[0]
    seq, width = r.u.shape
    keys = r.k.shape[0]
    half = width // 2
    heads = width // HEAD_DIM
    copies = Copies(r.sm)
    going = copies.choose(core == layer, both(r, "qkv"), r.wq)
    r.dqkv[:, 0:half] = r.dq[...]
    r.dqkv[0:keys, width : width + half] = r.dk[...]
    r.dqkv[0:keys, 2 * width : 2 * width + half] = r.dv[...]
    for head in range(heads // 2, heads):
        cols = [
            slice(part * width + head * HEAD_DIM, part * width + (head + 1) * HEAD_DIM)
            for part in range(3)
        ]
        head_back(
            r, head, r.er.at[head - heads // 2],
            r.dqkv.at[:, cols[0]], r.dqkv.at[0:keys, cols[1]], r.dqkv.at[0:keys, cols[2]],
        )
    for out_ref, begin in ((r.sd, (1 - core) * half), (r.kp, core * half)):
        rows = pl.ds(pl.multiple_of(begin, half), half)
        out_ref[:, 0:width] = dot_lt(r.u[:, rows], r.dqkv[:, 0:width]).astype(BF)
        out_ref[:, width:] = dot_lt(r.u[0:keys, rows], r.dqkv[0:keys, width:]).astype(BF)
    going.wait()


def late_heads(layer, core, early, weights, after=()):
    seq, width = early["q"].shape
    grads = (width // 2, 3 * width)
    return named(
        functools.partial(late_heads_kernel, layer),
        {"core": scalars(core)}
        | {
            name: near(early[name])
            for name in ("q", "k", "v", "u", "er", "dq", "dk", "dv", "dm", "ir")
        }
        | pairs(weights, "qkv"),
        {
            "sd": passed(grads),
            "kp": passed(grads),
            "dqkv": passed((seq, 3 * width)),
            "wq": passed(weights["qkv"][0].shape),
        },
        {"sm": DMA((1,))},
        "late",
        limit=14,
        flops=110_000_000_000,
        moved=16_000_000,
        after=after,
    )


def heads_kernel(layer, r):
    core = r.core[0]
    seq, width = r.u.shape
    keys = r.k.shape[0]
    copies = Copies(r.sm)
    going = copies.choose(core == layer, both(r, "qkv"), r.wq)
    for head in range(width // HEAD_DIM):
        cols = [
            slice(part * width + head * HEAD_DIM, part * width + (head + 1) * HEAD_DIM)
            for part in range(3)
        ]
        head_back(
            r, head, r.e.at[head],
            r.dqkv.at[:, cols[0]], r.dqkv.at[0:keys, cols[1]], r.dqkv.at[0:keys, cols[2]],
        )
    half = width // 2
    for out_ref, begin in ((r.sd, (1 - core) * half), (r.kp, core * half)):
        rows = pl.ds(pl.multiple_of(begin, half), half)
        out_ref[:, 0:width] = dot_lt(r.u[:, rows], r.dqkv[:, 0:width]).astype(BF)
        out_ref[:, width:] = dot_lt(r.u[0:keys, rows], r.dqkv[0:keys, width:]).astype(BF)
    going.wait()


def all_heads(layer, core, kept, dm, ir, weights, after=()):
    seq, width = kept["q"].shape
    grads = (width // 2, 3 * width)
    return named(
        functools.partial(heads_kernel, layer),
        {"core": scalars(core)}
        | {name: near(kept[name]) for name in ("q", "k", "v", "u", "e")}
        | {"dm": near(dm), "ir": near(ir)}
        | pairs(weights, "qkv"),
        {
            "sd": passed(grads),
            "kp": passed(grads),
            "dqkv": passed((seq, 3 * width)),
            "wq": passed(weights["qkv"][0].shape),
        },
        {"sm": DMA((1,))},
        "heads",
        limit=14,
        flops=220_000_000_000,
        moved=16_000_000,
        after=after,
    )


def input_gradient(dqkv, da, w, keys):
    seq, width = da.shape
    yield slice(0, keys), da[0:keys].astype(F32) + dot_rt(dqkv[0:keys], w[...])
    yield (
        slice(keys, seq),
        da[keys:seq].astype(F32) + dot_rt(dqkv[keys:seq, :width], w[:, :width]),
    )


BACK = ("x2", "s2", "sl", "x1", "s1", "mixed", "inv")


def turn_kernel(coming, r):
    own = r.core[0] == 0
    copies = Copies(r.sm)
    loads = {}
    for name in BACK:
        if name == "sl":
            loads["down"] = copies.choose(own, both(r, "down"), r.w_down)
        loads[name] = copies.start(getattr(r, name + "_in"), getattr(r, name))
        if name == "sl":
            loads["up"] = copies.choose(own, both(r, "up"), r.w_up)
    loads["out"] = copies.choose(own, both(r, "out"), r.w_out)
    going = bring(r, copies, coming)
    vec = jnp.where(own, r.va[...], r.vb[...])
    for rows, values in input_gradient(r.dqkv, r.da_in, r.wq, r.dqkv.shape[0] * 3 // 4):
        r.dy[rows] = values.astype(BF)

    def ready(*names):
        for name in names:
            loads.pop(name).wait()

    ready("x2", "s2")
    feed_back(
        vec, r.dy[...].astype(F32), r.x2, r.s2, r.sl, r.x1, r.s1, r.mixed, r.inv,
        r.w_down, r.w_up, r.w_out, [lambda: ready("down", "sl", "up"), lambda: ready(*list(loads))],
        r.df, r.dz, r.da, r.dm, r.ir, r.small,
    )
    for copy in going:
        copy.wait()


def turn(core, vecs, back, da, kept, weights, coming, after=()):
    seq, width = da.shape
    hidden = weights["up"][0].shape[1]
    wide, narrow = (seq, hidden), (seq, width)
    return named(
        functools.partial(turn_kernel, tuple(coming)),
        {
            "core": scalars(core),
            "va": (vecs[0], IN_VMEM),
            "vb": (vecs[1], IN_VMEM),
            "dqkv": near(back["dqkv"]),
            "da_in": near(da),
            "wq": near(back["wq"]),
        }
        | {name + "_in": held(kept[name]) for name in BACK}
        | pairs(weights, "down", "up", "out")
        | far(coming),
        {
            "df": passed(narrow),
            "dz": passed(wide),
            "da": passed(narrow),
            "dm": passed((width, seq)),
            "ir": passed((8, seq), F32),
            "small": passed((width, LANES)),
        }
        | brought(coming),
        {name: pltpu.VMEM(kept[name].shape, kept[name].dtype) for name in BACK}
        | {f"w_{name}": pltpu.VMEM(weights[name][0].shape, BF) for name in ("down", "up", "out")}
        | {"dy": pltpu.VMEM(narrow, BF), "sm": DMA((24,))},
        "turn",
        limit=36,
        flops=180_000_000_000,
        moved=16_000_000,
        after=after,
    )


def grads_kernel(r):
    feed_grads(
        r.core[0], r.g, r.df, r.h, r.dz, r.mixed, r.da, r.small, r.sd, r.kp
    )


def first_grads(core, back, after=()):
    seq, width = back["df"].shape
    hidden = back["dz"].shape[1]
    grads = (width // 2, 2 * hidden + width + LANES)
    return named(
        grads_kernel,
        {"core": scalars(core)}
        | {name: near(back[name + "_near"]) for name in ("h", "mixed", "g")}
        | {name: near(back[name]) for name in ("df", "dz", "da", "small")},
        {"sd": passed(grads), "kp": passed(grads)},
        {},
        "grads",
        limit=14,
        flops=120_000_000_000,
        moved=10_000_000,
        after=after,
    )


def last_kernel(r):
    seq, width = r.da.shape
    keys = seq * 3 // 4
    half = width // 2
    core = r.core[0]
    for out_ref, begin in ((r.sd, (1 - core) * half), (r.kp, core * half)):
        cols = pl.ds(pl.multiple_of(begin, half), half)
        out_ref[0:keys] = (
            r.da[0:keys, cols].astype(F32) + dot_rt(r.dqkv[0:keys], r.wq[cols])
        ).astype(BF)
        out_ref[keys:seq] = (
            r.da[keys:seq, cols].astype(F32)
            + dot_rt(r.dqkv[keys:seq, :width], r.wq[cols, :width])
        ).astype(BF)


def input_back(core, back, da, after=()):
    return named(
        last_kernel,
        {
            "core": scalars(core),
            "dqkv": near(back["dqkv"]),
            "da": near(da),
            "wq": near(back["wq"]),
        },
        {name: passed((da.shape[0], da.shape[1] // 2)) for name in ("sd", "kp")},
        {},
        "input",
        limit=8,
        flops=50_000_000_000,
        moved=6_000_000,
        after=after,
    )


def stages(count):
    bits = count.bit_length() - 1
    first = (bits - 1) // 3
    one = list(range(bits))
    two = one[first : 2 * first] + one[:first] + one[2 * first :]
    return list(zip(one, two))


def exchange(block, bits):
    count = lax.axis_size(DP)
    route = [
        (place * 2 + core, (place ^ 1 << bits[core]) * 2 + core)
        for place in range(count)
        for core in (0, 1)
    ]
    return lax.ppermute(block, (DP, SECTION), route)


def across(block):
    return lax.ppermute(block, SECTION, [(0, 1), (1, 0)])


def combine_kernel(stage, bits_ref, keep_ref, come_ref, *outs):
    if stage is None:
        outs[0][...] = (keep_ref[...].astype(F32) + come_ref[...].astype(F32)).astype(BF)
        return
    half = keep_ref.shape[0] // 2
    mine = bits_ref[stage] * half
    for out_ref, start in zip(outs, (half - mine, mine)):
        place = pl.ds(pl.multiple_of(start, TILE), half)
        out_ref[...] = (keep_ref[place].astype(F32) + come_ref[place].astype(F32)).astype(BF)


def combine(bits, stage, kp, come, after=()):
    rows, width = kp.shape
    outs = [shape((rows, width))] if stage is None else [shape((rows // 2, width))] * 2
    return call(
        functools.partial(combine_kernel, stage),
        "combine",
        [scalars(bits), (kp, IN_VMEM), (come, IN_VMEM)],
        [(out, IN_VMEM) for out in outs],
        limit=8,
        flops=STEP,
        after=after,
    )


def finish_kernel(*refs):
    out_ref = refs[-1]
    at = 0
    for keep_ref, come_ref in zip(refs[:-1:2], refs[1:-1:2]):
        width = keep_ref.shape[1]
        out_ref[:, at : at + width] = (
            keep_ref[...].astype(F32) + come_ref[...].astype(F32)
        ).astype(BF)
        at += width


def merge_kernel(stage, bits_ref, own_ref, come_ref, out_ref):
    rows = own_ref.shape[0]
    mine = bits_ref[stage] * rows
    out_ref[pl.ds(pl.multiple_of(mine, TILE), rows)] = own_ref[...]
    out_ref[pl.ds(pl.multiple_of(rows - mine, TILE), rows)] = come_ref[...]


def merge(bits, stage, own, come, after=()):
    rows, width = own.shape
    return call(
        functools.partial(merge_kernel, stage),
        "merge",
        [scalars(bits), (own, IN_VMEM), (come, IN_VMEM)],
        [(shape((2 * rows, width)), IN_VMEM)],
        limit=8,
        flops=STEP,
        after=after,
    )[0]


class Sums:
    def __init__(self, bits, arrays, halvings, turned):
        self.bits = bits
        self.turned = turned
        self.plan = stages(lax.axis_size(DP))
        if turned:
            first = (len(self.plan) - 1) // 3
            self.plan = (
                self.plan[first : 2 * first] + self.plan[:first] + self.plan[2 * first :]
            )
        self.halvings = halvings
        self.block = arrays["kp"]
        self.come = across(arrays["sd"])
        self.stage = 0
        self.halved = []
        self.doubling = False

    def place(self, stage):
        count = len(self.plan)
        first = (count - 1) // 3
        if self.turned and stage < 2 * first:
            stage = (stage + first) % (2 * first)
        return BITS + stage

    def left(self):
        return self.come is not None

    def step(self, after=()):
        if self.doubling:
            self.block = merge(self.bits, self.place(self.halved.pop()), self.block, self.come, after)
            return self.double()
        if self.stage == len(self.plan):
            (self.block,) = combine(self.bits, None, self.block, self.come, after)
            self.doubling = True
            return self.double()
        if self.stage >= self.halvings or self.block.shape[0] % (2 * TILE):
            (self.block,) = combine(self.bits, None, self.block, self.come, after)
            sd = self.block
        else:
            place = self.place(self.stage)
            sd, self.block = combine(self.bits, place, self.block, self.come, after)
            self.halved.append(self.stage)
        self.come = exchange(sd, self.plan[self.stage])
        self.stage += 1
        return (sd,)

    def double(self):
        self.come = exchange(self.block, self.plan[self.halved[-1]]) if self.halved else None
        return (self.block,)


def place_kernel(core_ref, keep_ref, come_ref, out_ref, mark_ref):
    rows = keep_ref.shape[0]
    mark_ref[...] = jnp.zeros_like(mark_ref)

    @pl.when(core_ref[0] == 0)
    def _():
        out_ref[0:rows] = keep_ref[...]
        out_ref[rows:] = come_ref[...]

    @pl.when(core_ref[0] == 1)
    def _():
        out_ref[0:rows] = come_ref[...]
        out_ref[rows:] = keep_ref[...]


def place_halves(core, kp, come, after=()):
    rows, width = kp.shape
    return call(
        place_kernel,
        "place",
        [scalars(core), (kp, IN_VMEM), (come, IN_VMEM)],
        [(shape((2 * rows, width)), IN_VMEM), (shape((8, LANES), F32), IN_VMEM)],
        limit=8,
        flops=STEP,
        after=after,
    )


def collect_kernel(count, mine, parts, r):
    half = r.one.shape[0]
    r.mark[...] = jnp.zeros_like(r.mark)

    def write(ref, begin):
        copies = Copies(r.sm)
        going = []
        at = 0
        for name, offset, width in parts:
            cols = slice(at, at + width)
            r.hold[:, cols] = ref[:, cols].astype(F32)
            target = getattr(r, name).at[0, offset + begin : offset + begin + half]
            going.append(copies.start(r.hold.at[:, cols], target))
            at += width
        for copy in going:
            copy.wait()

    def vectors(own_ref, come_ref, begin):
        at = sum(width for _, _, width in parts)
        for ref, place in ((own_ref, begin), (come_ref, half - begin)):
            small = ref[:, at:].astype(F32).T
            for row in range(count):
                width = r.out.shape[2]
                r.b_up[:, row * width + place : row * width + place + half] = small[row : row + 1]
            for row, name in enumerate(("bd", "g1", "c1", "g2", "c2")):
                getattr(r, name)[:, place : place + half] = small[count + row : count + row + 1]

    @pl.when(r.core[0] == 0)
    def _():
        if count:
            vectors(r.one_own, r.one, 0)
        write(r.one, 0 if mine else half)

    @pl.when(r.core[0] == 1)
    def _():
        if count:
            vectors(r.two_own, r.two, half)
        write(r.two, half if mine else 0)


def collect(core, one, two, outs, parts, name, after=(), begun=None, own=None, small=None):
    half = one.shape[0]
    begun = begun or {}
    ins = {"core": scalars(core), "one": (one, IN_VMEM), "two": (two, IN_VMEM)}
    if small:
        ins |= {"one_own": (own[0], IN_VMEM), "two_own": (own[1], IN_VMEM)}
    ins |= {name + "_begun": (array, ANYWHERE) for name, array in begun.items()}
    results = {name: (shape(dims, F32), ANYWHERE) for name, dims in outs.items()}
    results |= {name: (shape(dims, F32), IN_VMEM) for name, dims in (small or {}).items()}
    results["mark"] = (shape((8, LANES), F32), IN_VMEM)
    scratch = {
        "hold": pltpu.VMEM((half, sum(width for _, _, width in parts)), F32),
        "sm": DMA((len(parts),)),
    }
    names = list(ins) + list(results) + list(scratch)
    count = len(ins)
    first = count - len(begun)
    rows = small["b_up"][1] // small["bd"][1] if small else 0

    def run(*refs):
        collect_kernel(rows, not begun, parts, Refs(names, refs[:count] + refs[count + len(after) :]))

    values = pl.pallas_call(
        run,
        out_shape=[out for out, _ in results.values()],
        in_specs=[spec for _, spec in ins.values()] + [ANYWHERE] * len(after),
        out_specs=[spec for _, spec in results.values()],
        scratch_shapes=list(scratch.values()),
        input_output_aliases={first + place: place for place in range(len(begun))},
        compiler_params=pltpu.CompilerParams(vmem_limit_bytes=16 * MIB),
        cost_estimate=pl.CostEstimate(flops=STEP, bytes_accessed=0, transcendentals=0),
        name=name,
    )(*[array for array, _ in ins.values()], *after)
    return dict(zip(results, values))


def pack_kernel(r):
    copies = Copies(r.sm)
    names = ("b_up", "bd", "g1", "c1", "g2", "c2")
    going = [copies.start(getattr(r, name), getattr(r, name + "_hold")) for name in names]
    for copy in going:
        copy.wait()
    width = r.bd.shape[1]
    parts = r.b_up.shape[1] // width
    r.out[...] = jnp.zeros_like(r.out)
    for part in range(parts):
        r.out[part : part + 1] = r.b_up_hold[:, part * width : (part + 1) * width]
    for place, name in enumerate(names[1:]):
        r.out[parts + place : parts + place + 1] = getattr(r, name + "_hold")[...]


def pack(b_up, bd, g1, c1, g2, c2):
    arrays = {"b_up": b_up, "bd": bd, "g1": g1, "c1": c1, "g2": g2, "c2": c2}
    return named(
        pack_kernel,
        {name: held(array) for name, array in arrays.items()},
        {"out": (shape((8, bd.shape[1]), F32), IN_VMEM)},
        {name + "_hold": pltpu.VMEM(array.shape, F32) for name, array in arrays.items()}
        | {"sm": DMA((6,))},
        "pack",
        limit=4,
        flops=0,
        moved=20_000,
    )["out"]


def body(
    tokens, cotangent, lengths, train_counts,
    wq, w_out, w_up, b_up, w_down, bd, gain_one, bias_one, gain_two, bias_two,
):
    index = lax.axis_index(SECTION)
    place = lax.axis_index(DP)
    at_first = index == 0
    seq = tokens.shape[0] // lengths.shape[0]
    width = tokens.shape[1]
    hidden = w_up.shape[2]
    plan = stages(lax.axis_size(DP))
    first_bit = jnp.array([one for one, _ in plan], jnp.int32)
    other_bit = jnp.array([two for _, two in plan], jnp.int32)
    core = bits = jnp.concatenate(
        [
            index[None].astype(jnp.int32),
            place >> jnp.where(at_first, first_bit, other_bit) & 1,
        ]
    )
    weights = {"qkv": (wq[0], across(wq[0]))}
    vec = pack(b_up, bd, gain_one, bias_one, gain_two, bias_two)
    later = lax.optimization_barrier((w_out[0], w_up[0], w_down[0], vec))[:3]
    weights |= {name: (array, across(array)) for name, array in zip(("out", "up", "down"), later)}
    vecs = (vec, across(vec))

    first = attend_first(core, seq, train_counts, tokens, weights)
    kept = middle(core, train_counts, lengths, cotangent, vecs, first, weights)
    kept["u"] = kept["y"]
    kept_one = {name: kept[name] for name in KEPT} | {
        "mixed": kept["mo"], "inv": kept["io"],
        "q": first["q"], "k": first["k"], "v": first["v"], "e": first["e"],
    }

    def some(*names):
        return {name: kept_one[name] for name in names}

    sums = {A2: Sums(bits, kept, *PLANS[A2])}
    last_come = across(kept["ls"])
    vectors = {"b_up": (1, hidden)} | {
        name: (1, width) for name in ("bd", "g1", "c1", "g2", "c2")
    }
    feed_outs = {"up": (1, width, hidden), "out": (1, width, width), "down": (1, hidden, width)}
    feed_parts = [("up", 0, hidden), ("out", 0, width)]
    feed_parts += [("down", place * width, width) for place in range(hidden // width)]

    def come(one, two):
        return lax.ppermute(one, SECTION, [(1, 0)]), lax.ppermute(two, SECTION, [(0, 1)])

    mark = (kept["sd"],)
    for name in ORDER:
        if name == HEADS:
            two = all_heads(1, core, kept, kept["dm"], kept["ir"], weights, mark)
            sums[B2] = Sums(bits, two, *PLANS[B2])
            mark = (two["sd"],)
        elif name == TURN:
            back = turn(
                core, vecs, two, kept["da"], kept_one, weights, some("h", "g", "mixed"), mark
            )
            mark = (back["df"],)
        elif name == GRADS:
            grads = first_grads(core, back, mark)
            sums[A1] = Sums(bits, grads, *PLANS[A1])
            mark = (grads["sd"],)
        elif name == EARLY:
            early = early_heads(core, kept_one, back["dm"], back["ir"], tokens, mark)
            mark = (early["dq"],)
        elif name == LATE:
            one = late_heads(0, core, early, weights, mark)
            sums[B1] = Sums(bits, one, *PLANS[B1])
            mark = (one["sd"],)
        elif name == INPUT:
            du = input_back(core, one, back["da"], mark)
            du_come = across(du["sd"])
            mark = (du["sd"],)
        elif name == OUT:
            output, *mark = place_halves(core, kept["lk"], last_come, mark)
        elif name == IN:
            grad_tokens, *mark = place_halves(core, du["kp"], du_come, mark)
        elif name == OWN:
            while sums[A1].left():
                mark = sums[A1].step(mark)
            while sums[A2].left():
                mark = sums[A2].step(mark)
            fed = sums[A1].block, sums[A2].block
            fed_come = come(*fed)
            feed_begun = collect(core, *fed, feed_outs, feed_parts, "own", mark)
            mark = (feed_begun.pop("mark"),)
        elif name == COME:
            feed_done = collect(
                core, *fed_come, feed_outs, feed_parts, "come", mark, feed_begun, fed, vectors
            )
            mark = (feed_done.pop("mark"),)
        elif sums[name].left():
            mark = sums[name].step(mark)
    qkv_outs, qkv_parts = {"qkv": (1, width, 3 * width)}, [("qkv", 0, 3 * width)]
    for name in (B2, B1):
        while sums[name].left():
            mark = sums[name].step(mark)
    qkv = sums[B1].block, sums[B2].block
    qkv_come = come(*qkv)
    qkv_begun = collect(core, *qkv, qkv_outs, qkv_parts, "own", mark)
    del qkv_begun["mark"]
    grad_w_qkv = collect(core, *qkv_come, qkv_outs, qkv_parts, "come", (), qkv_begun)["qkv"]
    grad_w_up, grad_w_out, grad_w_down, *grad_vectors = feed_done.values()
    grad_b_up, grad_b_down, *grad_norms = grad_vectors
    return (
        output,
        grad_tokens,
        grad_w_qkv,
        grad_w_out,
        grad_w_up,
        grad_b_up,
        grad_w_down,
        grad_b_down,
        *grad_norms,
    )


def solution(mesh):
    matrix = P(SECTION, None, None)
    vector = P(SECTION, None)
    weights = (matrix, matrix, matrix, vector, matrix, vector, vector, vector, vector, vector)
    rows = P(DP, None)
    halves = P(DP, SECTION)
    return jax.shard_map(
        body,
        mesh=mesh,
        in_specs=(rows, rows, P(DP), P(DP)) + weights,
        out_specs=(halves, halves) + weights,
        check_vma=False,
    )
```
